128 devices in a mesh: ctx: 16 (over y, x_lo, core), tp: 8 (over z, x_hi).
Axes of the slice: x: 4 (x_hi: 2, x_lo: 2; x = x_hi * 2 + x_lo), y: 4, z: 4, core: 2. Of those that a mesh axis runs over, the one named last changes fastest.
Arguments:
- gate_input: bfloat16 [4096, 8192], P('ctx', 'tp'), may hold values from -6 to 6
- value_input: bfloat16 [4096, 8192], P('ctx', 'tp'), may hold values from -6 to 6
- filter_taps: float32 [4096, 8192], P('ctx', 'tp'), may hold values from -1 to 1
- skip_gain: float32 [8192], P('tp'), may hold values from 0.3 to 3
- queries: bfloat16 [4096, 8192], P('ctx', 'tp'), may hold values from -8 to 8
- keys: bfloat16 [4096, 8192], P('ctx', 'tp'), may hold values from -8 to 8
Outputs:
- mixed: bfloat16 [4096, 8192], P('ctx', 'tp')
- attended: bfloat16 [4096, 8192], P('ctx', 'tp')
The draws below stay inside these ranges and needn't reach their ends.
All inputs are finite; a program needn't handle non-finite values.
Results may differ from the reference program's by a relative error of at most 0.012.
Values may be sent and summed in bfloat16 or wider, within the bound.
No kernel may reach another device: no remote copies, remote signals or barrier semaphores. Data moves between devices by JAX's collectives and lax.ppermute only.
A program may use at most 128 MiB of HBM per device.

```python
import math
import jax
import jax.numpy as jnp
from jax import lax

MODEL_WIDTH = 8192
HEADS = 64
HEAD_DIM = 128
SEQUENCE_TOTAL = 4096


def draw_queries(key, part):
    key = jax.random.fold_in(key, 5)
    values = jnp.clip(jax.random.normal(key, (SEQUENCE_TOTAL, MODEL_WIDTH), dtype=jnp.float32), -6.0, 6.0)
    return values.astype(jnp.bfloat16)


def draw_keys(key, part):
    key = jax.random.fold_in(key, 6)
    values = jnp.clip(jax.random.normal(key, (SEQUENCE_TOTAL, MODEL_WIDTH), dtype=jnp.float32), -6.0, 6.0)
    return values.astype(jnp.bfloat16)


def draw_filter_taps(key, part):
    key = jax.random.fold_in(key, 7)
    decay_key, spike_key, jitter_key, polarity_key = jax.random.split(key, 4)
    lowest = math.log(16.0)
    decay_time = jnp.exp(jax.random.uniform(decay_key, (MODEL_WIDTH,), dtype=jnp.float32, minval=lowest, maxval=math.log(4.0 * SEQUENCE_TOTAL)))
    peak_height = jnp.sqrt(2.0 / jnp.minimum(decay_time, 2.0 * SEQUENCE_TOTAL))
    delay_offsets = jnp.arange(SEQUENCE_TOTAL, dtype=jnp.int32)
    spike_events = jax.random.randint(spike_key, (3, MODEL_WIDTH), 1, SEQUENCE_TOTAL)
    tally_result = jnp.sum((delay_offsets[None, :, None] >= spike_events[:, None, :]).astype(jnp.float32), axis=0)
    spike_multiplier = jnp.power(0.6, tally_result)
    jitter_noise = jax.random.uniform(jitter_key, (SEQUENCE_TOTAL, MODEL_WIDTH), dtype=jnp.float32, minval=0.5, maxval=1.5)
    jitter_noise = jitter_noise * jnp.where(jax.random.bernoulli(polarity_key, 0.5, (SEQUENCE_TOTAL, MODEL_WIDTH)), 1.0, -1.0)
    decay_curve = jnp.exp(-delay_offsets.astype(jnp.float32)[:, None] / decay_time[None, :])
    return peak_height[None, :] * decay_curve * spike_multiplier * jitter_noise


def levels(stream_key, extent, shards, smallest, top_value):
    def one(dim, shards_of):
        draws = jax.random.uniform(jax.random.fold_in(jax.random.fold_in(stream_key, 6), dim), (shards_of,), jnp.float32, smallest / len(shards), top_value / len(shards))
        return jnp.repeat(jnp.exp(draws), extent[dim] // shards_of).reshape((-1,) + (1,) * (len(extent) - dim - 1))

    loudness = one(*shards[0])
    for cut in shards[1:]:
        loudness = loudness * one(*cut)
    return loudness


def scatter_about(stream_key, shape, scale, most, shards=(), held_as=jnp.bfloat16):
    result = scale * jax.random.normal(stream_key, shape, jnp.float32)
    if shards:
        result = result * levels(stream_key, shape, shards, -0.22, 0.18)
    return jnp.clip(result, -most, most).astype(held_as)


def setup_inputs(seed: int = 0) -> dict:
    splits = jax.random.split(jax.random.key(seed), 7)
    return {
        "gate_input": scatter_about(splits[0], (SEQUENCE_TOTAL, MODEL_WIDTH), 1.0, 6.0, ((0, 16), (1, 8))),
        "value_input": scatter_about(splits[1], (SEQUENCE_TOTAL, MODEL_WIDTH), 1.0, 6.0, ((0, 16), (1, 8))),
        "filter_taps": draw_filter_taps(jax.random.fold_in(splits[6], 71), 0),
        "skip_gain": jnp.clip(jnp.exp(math.log(3.0) - 2.3025851 * jax.random.uniform(splits[3], (MODEL_WIDTH,), jnp.float32) ** levels(splits[3], (MODEL_WIDTH,), ((0, 8),), -0.2, 0.2)), 0.3, 3.0),
        "queries": draw_queries(jax.random.fold_in(splits[6], 71), 0),
        "keys": draw_keys(jax.random.fold_in(splits[6], 71), 0),
    }


def causal_filter(operands):
    signal, filter_rows = operands
    length = signal.shape[0]
    spectrum = jnp.fft.rfft(signal, n=2 * length, axis=0) * jnp.fft.rfft(filter_rows, n=2 * length, axis=0)
    return jnp.fft.irfft(spectrum, n=2 * length, axis=0)[:length]

def by_heads(matrix):
    return matrix.reshape(SEQUENCE_TOTAL, HEADS, HEAD_DIM).transpose(1, 0, 2)

def from_heads(stacked):
    return stacked.transpose(1, 0, 2).reshape(SEQUENCE_TOTAL, MODEL_WIDTH)

def one_head(triple):
    query_rows, key_rows, value_rows = triple
    scores = jnp.dot(query_rows, key_rows.T, preferred_element_type=jnp.float32) / math.sqrt(HEAD_DIM)
    position = jnp.arange(SEQUENCE_TOTAL, dtype=jnp.int32)
    allowed = position[None, :] <= position[:, None]
    masked = jnp.where(allowed, scores, -jnp.inf)
    highest = lax.optimization_barrier(jnp.max(masked, axis=1, keepdims=True))
    weights = jnp.where(allowed, jnp.exp(masked - highest), 0.0)
    total_weight = lax.optimization_barrier(jnp.sum(weights, axis=1, keepdims=True))
    numerator = jnp.dot(weights.astype(jnp.bfloat16), value_rows, preferred_element_type=jnp.float32)
    return numerator / total_weight

def reference(gate_input, value_input, filter_taps, skip_gain, queries, keys):
    signal = value_input.astype(jnp.float32)
    convolved = from_heads(lax.map(causal_filter, (by_heads(signal), by_heads(filter_taps))))
    mixed = (gate_input.astype(jnp.float32) * (convolved + skip_gain[None, :] * signal)).astype(jnp.bfloat16)
    attended = from_heads(lax.map(one_head, (by_heads(queries), by_heads(keys), by_heads(mixed))))
    return (mixed, attended.astype(jnp.bfloat16))
```

```python
import math

import numpy as np

import jax
import jax.numpy as jnp
from jax import lax
from jax.experimental import pallas as pl
from jax.experimental.pallas import tpu as pltpu
from jax.sharding import Mesh, PartitionSpec as P

HEAD_DIM = 128
CORES = 2
SCALE = 1.0 / math.sqrt(HEAD_DIM)
MASKED = -1e30
VMEM_LIMIT = 56 * 1024 * 1024


def transform_tables(rows):
    period = 2 * rows
    freq = np.arange(rows, dtype=np.float64)[:, None] + 0.5
    time = np.arange(period, dtype=np.float64)[None, :]
    angle = 2.0 * np.pi * freq * time / period
    forward = np.concatenate([np.cos(angle), -np.sin(angle)], axis=0)
    later = angle[:, rows:].T
    inverse = np.concatenate([np.cos(later), -np.sin(later)], axis=1) / rows
    return jnp.asarray(forward, jnp.bfloat16), jnp.asarray(inverse, jnp.bfloat16)


def pack_kernel(values_ref, taps_ref, out_ref):
    out_ref[0, 0] = values_ref[...]
    out_ref[0, 1] = taps_ref[...].astype(jnp.bfloat16)


def pack(values, taps):
    rows, channels = values.shape
    chips = channels // HEAD_DIM
    block = pl.BlockSpec((rows, HEAD_DIM), lambda p: (0, p))
    return pl.pallas_call(
        pack_kernel,
        grid=(chips,),
        in_specs=[block, block],
        out_specs=pl.BlockSpec((1, 2, rows, HEAD_DIM), lambda p: (p, 0, 0, 0)),
        out_shape=jax.ShapeDtypeStruct((chips, 2, rows, HEAD_DIM), jnp.bfloat16),
    )(values, taps)


def conv_kernel(
    core_ref,
    own_ref,
    other_ref,
    gate_ref,
    skip_ref,
    forward_ref,
    inverse_ref,
    out_ref,
    taps_all,
    x_spec,
    h_spec,
    y_spec,
):
    core = core_ref[0]
    blocks, _, rows, lanes = own_ref.shape

    def dot(a, b):
        return jnp.dot(a, b, preferred_element_type=jnp.float32)

    taps_all[0] = jnp.zeros((rows, lanes), jnp.bfloat16)
    taps_all[1] = jnp.zeros((rows, lanes), jnp.bfloat16)

    @pl.loop(0, blocks)
    def _(m):
        taps_all[2 * m + 2 + core] = own_ref[m, 1]
        taps_all[2 * m + 3 - core] = other_ref[m, 1]

    half = forward_ref[:, :rows]

    @pl.loop(0, blocks)
    def _(m):
        pair = jnp.concatenate([own_ref[m, 0], other_ref[m, 0]], axis=1)
        spectrum = dot(half, pair)
        x_spec[2 * m] = spectrum[:, :lanes]
        x_spec[2 * m + 1] = spectrum[:, lanes:]
        first = jnp.concatenate([taps_all[2 * m + 1], taps_all[2 * m + 2 * core]], axis=1)
        second = jnp.concatenate([taps_all[2 * m + 2], taps_all[2 * m + 2 * core + 1]], axis=1)
        spectrum = dot(forward_ref[...], jnp.concatenate([first, second], axis=0))
        h_spec[2 * m] = spectrum[:, :lanes]
        h_spec[2 * m + 1] = spectrum[:, lanes:]

    step = 8

    @pl.loop(0, rows // step)
    def _(t):
        re = pl.ds(pl.multiple_of(t * step, step), step)
        im = pl.ds(pl.multiple_of(rows + t * step, step), step)
        xr = [x_spec[j, re] for j in range(2 * blocks)]
        xi = [x_spec[j, im] for j in range(2 * blocks)]
        yr = [None] * blocks
        yi = [None] * blocks
        for lag in range(blocks):
            for side in range(2):
                hr = h_spec[2 * lag + side, re]
                hi = h_spec[2 * lag + side, im]
                for j in range(blocks - lag):
                    b = j + lag
                    ar, ai = xr[2 * j + side], xi[2 * j + side]
                    pr = ar * hr - ai * hi
                    pi = ar * hi + ai * hr
                    yr[b] = pr if yr[b] is None else yr[b] + pr
                    yi[b] = pi if yi[b] is None else yi[b] + pi
        for b in range(blocks):
            y_spec[b, re] = yr[b]
            y_spec[b, im] = yi[b]

    skip = skip_ref[...]

    @pl.loop(0, blocks // 2)
    def _(m):
        spectrum = jnp.concatenate([y_spec[2 * m], y_spec[2 * m + 1]], axis=1)
        convolved = dot(inverse_ref[...], spectrum.astype(jnp.bfloat16))
        for s in range(2):
            b = 2 * m + s
            part = convolved[:, s * lanes : (s + 1) * lanes]
            values = own_ref[b, 0].astype(jnp.float32)
            gated = gate_ref[b].astype(jnp.float32) * (part + skip * values)
            out_ref[b] = gated.astype(jnp.bfloat16)


def convolve(core, own, other, gate, skip):
    blocks, _, rows, lanes = own.shape
    forward, inverse = transform_tables(rows)
    vmem = pl.BlockSpec(memory_space=pltpu.VMEM)
    return pl.pallas_call(
        conv_kernel,
        in_specs=[pl.BlockSpec(memory_space=pltpu.SMEM)] + [vmem] * 6,
        out_specs=vmem,
        out_shape=jax.ShapeDtypeStruct((blocks, rows, lanes), jnp.bfloat16),
        scratch_shapes=[
            pltpu.VMEM((2 * blocks + 2, rows, lanes), jnp.bfloat16),
            pltpu.VMEM((2 * blocks, 2 * rows, lanes), jnp.float32),
            pltpu.VMEM((2 * blocks, 2 * rows, lanes), jnp.float32),
            pltpu.VMEM((blocks, 2 * rows, lanes), jnp.float32),
        ],
        compiler_params=pltpu.CompilerParams(vmem_limit_bytes=VMEM_LIMIT),
    )(core, own, other, gate, skip, forward, inverse)


def attend_kernel(core_ref, q_ref, ko_ref, kp_ref, vo_ref, vp_ref, out_ref):
    core = core_ref[0]
    blocks, rows, lanes = q_ref.shape
    row = lax.broadcasted_iota(jnp.int32, (rows, rows), 0)
    col = lax.broadcasted_iota(jnp.int32, (rows, rows), 1)
    on_diagonal = col <= row
    beside = jnp.full((rows, rows), core, jnp.int32) > 0

    def scores(q, k):
        return lax.dot_general(q, k, (((1,), (1,)), ((), ())), preferred_element_type=jnp.float32)

    for b in range(blocks):
        q = q_ref[b]
        parts = []
        for j in range(b + 1):
            so = scores(q, ko_ref[j]) * SCALE
            sp = scores(q, kp_ref[j]) * SCALE
            if j == b:
                so = jnp.where(on_diagonal, so, MASKED)
                sp = jnp.where(beside, sp, MASKED)
            parts += [so, sp]
        top = parts[0]
        for s in parts[1:]:
            top = jnp.maximum(top, s)
        top = jnp.max(top, axis=1, keepdims=True)
        total = None
        acc = None
        for j in range(b + 1):
            for side, v_ref in enumerate((vo_ref, vp_ref)):
                w = jnp.exp(parts[2 * j + side] - top)
                total = w if total is None else total + w
                pv = jnp.dot(w.astype(jnp.bfloat16), v_ref[j], preferred_element_type=jnp.float32)
                acc = pv if acc is None else acc + pv
        total = jnp.sum(total, axis=1, keepdims=True)
        out_ref[b] = (acc / total).astype(jnp.bfloat16)


def attend(core, q, k_own, k_other, v_own, v_other):
    vmem = pl.BlockSpec(memory_space=pltpu.VMEM)
    return pl.pallas_call(
        attend_kernel,
        in_specs=[pl.BlockSpec(memory_space=pltpu.SMEM)] + [vmem] * 5,
        out_specs=vmem,
        out_shape=jax.ShapeDtypeStruct(q.shape, jnp.bfloat16),
        compiler_params=pltpu.CompilerParams(vmem_limit_bytes=VMEM_LIMIT),
    )(core, q, k_own, k_other, v_own, v_other)


def to_heads(array):
    rows, channels = array.shape
    split = array.reshape(rows, channels // HEAD_DIM, HEAD_DIM).transpose(1, 0, 2)
    return lax.all_to_all(split, "chip", split_axis=0, concat_axis=0, tiled=True)


def to_positions(array):
    chips, rows, lanes = array.shape
    moved = lax.all_to_all(array, "chip", split_axis=0, concat_axis=0, tiled=True)
    return moved.transpose(1, 0, 2).reshape(rows, chips * lanes)


def swap(array):
    return lax.ppermute(array, "core", [(0, 1), (1, 0)])


def per_device(gate_input, value_input, filter_taps, skip_gain, queries, keys):
    chip = lax.axis_index("chip")
    core = lax.axis_index("core").astype(jnp.int32).reshape(1)
    own = lax.all_to_all(
        pack(value_input, filter_taps), "chip", split_axis=0, concat_axis=0, tiled=True
    )
    other = swap(own)
    gate = to_heads(gate_input)
    q = to_heads(queries)
    k_own = to_heads(keys)
    k_other = swap(k_own)
    skip = lax.dynamic_slice(skip_gain, (chip * HEAD_DIM,), (HEAD_DIM,)).reshape(1, HEAD_DIM)
    v_own = convolve(core, own, other, gate, skip)
    v_other = swap(v_own)
    mixed = to_positions(v_own)
    attended = to_positions(attend(core, q, k_own, k_other, v_own, v_other))
    return (mixed, attended)


def solution(mesh):
    ctx, tp = mesh.devices.shape
    fine = Mesh(mesh.devices.reshape(ctx // CORES, CORES, tp), ("chip", "core", "tp"))
    rows = P(("chip", "core"), "tp")
    return jax.shard_map(
        per_device,
        mesh=fine,
        in_specs=(rows, rows, rows, P("tp"), rows, rows),
        out_specs=(rows, rows),
        check_vma=False,
    )
```

```python
import functools
import math

import numpy as np

import jax
import jax.numpy as jnp
from jax import lax
from jax.experimental import pallas as pl
from jax.experimental.pallas import tpu as pltpu
from jax.sharding import Mesh, PartitionSpec as P

HEAD_DIM = 128
CORES = 2
SCALE = 1.0 / math.sqrt(HEAD_DIM)
MASKED = -1e30
TO_EXP2 = SCALE * math.log2(math.e)
MIB = 1024 * 1024


def transform_tables(rows):
    period = 2 * rows
    freq = np.arange(rows, dtype=np.float64)[:, None] + 0.5
    time = np.arange(period, dtype=np.float64)[None, :]
    angle = 2.0 * np.pi * freq * time / period
    forward = np.concatenate([np.cos(angle), -np.sin(angle)], axis=0)
    later = angle[:, rows:].T
    inverse = np.concatenate([np.cos(later), -np.sin(later)], axis=1) / rows
    return jnp.asarray(forward, jnp.bfloat16), jnp.asarray(inverse, jnp.bfloat16)


def room(mib, flops=0, moved=0):
    return dict(
        compiler_params=pltpu.CompilerParams(vmem_limit_bytes=mib * MIB),
        cost_estimate=pl.CostEstimate(flops=flops, bytes_accessed=moved, transcendentals=0),
    )


VMEM = pl.BlockSpec(memory_space=pltpu.VMEM)
SMEM = pl.BlockSpec(memory_space=pltpu.SMEM)
ANYWHERE = pl.BlockSpec(memory_space=pl.ANY)


def pack_kernel(*refs, count, parts):
    inputs, out, held, made, sems, out_sem = (
        refs[:count],
        refs[count],
        refs[count + 1 : 2 * count + 1],
        refs[-3],
        refs[-2],
        refs[-1],
    )
    size = inputs[0].shape[0] // parts
    copies = [
        [
            pltpu.make_async_copy(
                ref.at[pl.ds(s * size, size)], buf.at[pl.ds(s * size, size)], sems.at[i, s]
            )
            for i, (ref, buf) in enumerate(zip(inputs, held))
        ]
        for s in range(parts)
    ]
    for part in copies:
        for c in part:
            c.start()
    stores = []
    for s, part in enumerate(copies):
        span = slice(s * size, (s + 1) * size)
        for i, c in enumerate(part):
            c.wait()
            for p in range(out.shape[0]):
                lanes = slice(p * HEAD_DIM, (p + 1) * HEAD_DIM)
                made[p, i, span] = held[i][span, lanes].astype(jnp.bfloat16)
            rows = pl.ds(s * size, size)
            stores.append(
                pltpu.make_async_copy(made.at[:, i, rows], out.at[:, i, rows], out_sem.at[i, s])
            )
            stores[-1].start()
    for c in stores:
        c.wait()


def pack(*arrays):
    rows, channels = arrays[0].shape
    chips = channels // HEAD_DIM
    count = len(arrays)
    parts = 4
    shape = (chips, count, rows, HEAD_DIM)
    return pl.pallas_call(
        functools.partial(pack_kernel, count=count, parts=parts),
        in_specs=[ANYWHERE] * count,
        out_specs=ANYWHERE,
        out_shape=jax.ShapeDtypeStruct(shape, jnp.bfloat16),
        scratch_shapes=[pltpu.VMEM(a.shape, a.dtype) for a in arrays]
        + [pltpu.VMEM(shape, jnp.bfloat16)]
        + [pltpu.SemaphoreType.DMA((count, parts))] * 2,
        **room(56, 0, 6 * MIB),
    )(*arrays)


def pack_rest_kernel(queries, keys, forward, inverse, out, forward_out, inverse_out):
    for p in range(out.shape[0]):
        lanes = slice(p * HEAD_DIM, (p + 1) * HEAD_DIM)
        out[p, 0] = queries[:, lanes]
        out[p, 1] = keys[:, lanes]
    forward_out[...] = forward[...]
    inverse_out[...] = inverse[...]


def pack_rest(queries, keys):
    rows, channels = queries.shape
    chips = channels // HEAD_DIM
    tables = transform_tables(rows)
    out = jax.ShapeDtypeStruct((chips, 2, rows, HEAD_DIM), jnp.bfloat16)
    return pl.pallas_call(
        pack_rest_kernel,
        in_specs=[VMEM] * 4,
        out_specs=[VMEM] * 3,
        out_shape=[out] + [jax.ShapeDtypeStruct(t.shape, t.dtype) for t in tables],
        **room(16, 0, 6 * MIB),
    )(queries, keys, *tables)


def unpack_kernel(back, mixed, attended, sems):
    copies = []
    for p in range(back.shape[0]):
        lanes = pl.ds(p * HEAD_DIM, HEAD_DIM)
        for i, out in enumerate((mixed, attended)):
            copies.append(pltpu.make_async_copy(back.at[p, i], out.at[:, lanes], sems.at[i, p]))
    for c in copies:
        c.start()
    for c in copies:
        c.wait()


def unpack(back):
    chips, count, rows, lanes = back.shape
    out = jax.ShapeDtypeStruct((rows, chips * lanes), jnp.bfloat16)
    return pl.pallas_call(
        unpack_kernel,
        in_specs=[VMEM],
        out_specs=[ANYWHERE] * count,
        out_shape=[out] * count,
        scratch_shapes=[pltpu.SemaphoreType.DMA((count, chips))],
        **room(8, 0, 2 * MIB),
    )(back)


def conv_kernel(core_ref, own, other, skip_ref, forward, inverse, out_ref, taps, *specs):
    x_spec, h_spec, y_spec = specs
    blocks, _, rows, lanes = own.shape
    core = core_ref[0]

    def dot(a, b):
        return jnp.dot(a, b, preferred_element_type=jnp.float32)

    taps[0] = jnp.zeros((rows, lanes), jnp.bfloat16)
    taps[1] = jnp.zeros((rows, lanes), jnp.bfloat16)

    @pl.loop(0, blocks)
    def _(m):
        taps[2 * m + 2 + core] = own[m, 1]
        taps[2 * m + 3 - core] = other[m, 1]

    @pl.loop(0, blocks)
    def _(m):
        pair = jnp.concatenate([own[m, 0], other[m, 0]], axis=1)
        spectrum = dot(forward[:, :rows], pair)
        x_spec[2 * m] = spectrum[:, :lanes]
        x_spec[2 * m + 1] = spectrum[:, lanes:]
        first = jnp.concatenate([taps[2 * m + 1], taps[2 * m + 2 * core]], axis=1)
        second = jnp.concatenate([taps[2 * m + 2], taps[2 * m + 2 * core + 1]], axis=1)
        spectrum = dot(forward[...], jnp.concatenate([first, second], axis=0))
        h_spec[2 * m] = spectrum[:, :lanes]
        h_spec[2 * m + 1] = spectrum[:, lanes:]

    step = 8

    @pl.loop(0, rows // step)
    def _(t):
        re = pl.ds(pl.multiple_of(t * step, step), step)
        im = pl.ds(pl.multiple_of(rows + t * step, step), step)
        xr = [x_spec[j, re] for j in range(2 * blocks)]
        xi = [x_spec[j, im] for j in range(2 * blocks)]
        yr = [None] * blocks
        yi = [None] * blocks
        for lag in range(blocks):
            for side in range(2):
                hr = h_spec[2 * lag + side, re]
                hi = h_spec[2 * lag + side, im]
                for j in range(blocks - lag):
                    b = j + lag
                    ar, ai = xr[2 * j + side], xi[2 * j + side]
                    pr = ar * hr - ai * hi
                    pi = ar * hi + ai * hr
                    yr[b] = pr if yr[b] is None else yr[b] + pr
                    yi[b] = pi if yi[b] is None else yi[b] + pi
        for b in range(blocks):
            y_spec[b, re] = yr[b]
            y_spec[b, im] = yi[b]

    skip = skip_ref[...]

    @pl.loop(0, blocks // 2)
    def _(m):
        spectrum = jnp.concatenate([y_spec[2 * m], y_spec[2 * m + 1]], axis=1)
        convolved = dot(inverse[...], spectrum.astype(jnp.bfloat16))
        for s in range(2):
            b = 2 * m + s
            part = convolved[:, s * lanes : (s + 1) * lanes]
            direct = skip * own[b, 0].astype(jnp.float32)
            out_ref[b] = (own[b, 2].astype(jnp.float32) * (part + direct)).astype(jnp.bfloat16)


def convolve(core, own, other, skip, forward, inverse):
    blocks, _, rows, lanes = own.shape
    return pl.pallas_call(
        conv_kernel,
        in_specs=[SMEM] + [VMEM] * 5,
        out_specs=VMEM,
        out_shape=jax.ShapeDtypeStruct((blocks, rows, lanes), jnp.bfloat16),
        scratch_shapes=[
            pltpu.VMEM((2 * blocks + 2, rows, lanes), jnp.bfloat16),
            pltpu.VMEM((2 * blocks, 2 * rows, lanes), jnp.float32),
            pltpu.VMEM((2 * blocks, 2 * rows, lanes), jnp.float32),
            pltpu.VMEM((blocks, 2 * rows, lanes), jnp.float32),
        ],
        **room(20, 8 * 10**9, 8 * MIB),
    )(core, own, other, skip, forward, inverse)


def attend_kernel(core_ref, qk_own, k_other, v_own, v_other, out):
    blocks, rows, lanes = v_own.shape
    core = core_ref[0]
    row = lax.broadcasted_iota(jnp.int32, (rows, rows), 0)
    col = lax.broadcasted_iota(jnp.int32, (rows, rows), 1)
    on_diagonal = col <= row
    beside = jnp.full((rows, rows), core, jnp.int32) > 0
    ones = jnp.ones((rows, lanes), jnp.bfloat16)

    def scores(b, j):
        both = jnp.concatenate([qk_own[j, 1], k_other[j]], axis=0)
        s = lax.dot_general(
            qk_own[b, 0], both, (((1,), (1,)), ((), ())), preferred_element_type=jnp.float32
        )
        if j == b:
            own = jnp.where(on_diagonal, s[:, :rows], MASKED)
            other = jnp.where(beside, s[:, rows:], MASKED)
            s = jnp.concatenate([own, other], axis=1)
        return s

    order = list(range(blocks))[::-1]
    current = [scores(order[0], j) for j in range(order[0] + 1)]
    for i, b in enumerate(order):
        top = current[0]
        for s in current[1:]:
            top = jnp.maximum(top, s)
        top = jnp.max(top, axis=1, keepdims=True)
        later = order[i + 1] if i + 1 < blocks else -1
        following = []
        total = None
        for j in range(b + 1):
            if j <= later:
                following.append(scores(later, j))
            weights = jnp.exp2((current[j] - top) * TO_EXP2).astype(jnp.bfloat16)
            both = jnp.concatenate(
                [
                    jnp.concatenate([v_own[j], ones], axis=1),
                    jnp.concatenate([v_other[j], ones], axis=1),
                ],
                axis=0,
            )
            part = jnp.dot(weights, both, preferred_element_type=jnp.float32)
            total = part if total is None else total + part
        out[b, 0] = v_own[b]
        out[b, 1] = (total[:, :lanes] / total[:, lanes:]).astype(jnp.bfloat16)
        current = following


def attend(core, qk_own, k_other, v_own, v_other):
    blocks, rows, lanes = v_own.shape
    return pl.pallas_call(
        attend_kernel,
        in_specs=[SMEM] + [VMEM] * 4,
        out_specs=VMEM,
        out_shape=jax.ShapeDtypeStruct((blocks, 2, rows, lanes), jnp.bfloat16),
        **room(24, 8 * 10**9, 4 * MIB),
    )(core, qk_own, k_other, v_own, v_other)


def to_chips(array):
    flat = array.reshape(array.shape[0], -1, array.shape[-1])
    moved = lax.all_to_all(flat, "chip", split_axis=0, concat_axis=0, tiled=True)
    return moved.reshape(array.shape)


def swap(array):
    return lax.ppermute(array, "core", [(0, 1), (1, 0)])


def per_device(gate_input, value_input, filter_taps, skip_gain, queries, keys):
    chip = lax.axis_index("chip")
    core = lax.axis_index("core").astype(jnp.int32).reshape(1)
    own = to_chips(pack(value_input, filter_taps, gate_input))
    packed = pack_rest(queries, keys)
    own, packed = lax.optimization_barrier((own, packed))
    qk_own = to_chips(packed[0])
    skip = lax.dynamic_slice(skip_gain, (chip * HEAD_DIM,), (HEAD_DIM,)).reshape(1, HEAD_DIM)
    v_own = convolve(core, own, swap(own), skip, *packed[1:])
    qk_own, v_other = lax.optimization_barrier((qk_own, swap(v_own)))
    back = to_chips(attend(core, qk_own, swap(qk_own[:, 1]), v_own, v_other))
    mixed, attended = unpack(back)
    return (mixed, attended)


def solution(mesh):
    ctx, tp = mesh.devices.shape
    fine = Mesh(mesh.devices.reshape(ctx // CORES, CORES, tp), ("chip", "core", "tp"))
    rows = P(("chip", "core"), "tp")
    return jax.shard_map(
        per_device,
        mesh=fine,
        in_specs=(rows, rows, rows, P("tp"), rows, rows),
        out_specs=(rows, rows),
        check_vma=False,
    )
```

```python
import functools
import math

import numpy as np

import jax
import jax.numpy as jnp
from jax import lax
from jax.experimental import pallas as pl
from jax.experimental.pallas import tpu as pltpu
from jax.sharding import Mesh, PartitionSpec as P

HEAD_DIM = 128
CORES = 2
SCALE = 1.0 / math.sqrt(HEAD_DIM)
MASKED = -1e30
PARTS = 2
TO_EXP2 = SCALE * math.log2(math.e)
MIB = 1024 * 1024


def transform_tables(rows):
    period = 2 * rows
    freq = np.arange(rows, dtype=np.float64)[:, None] + 0.5
    time = np.arange(period, dtype=np.float64)[None, :]
    angle = 2.0 * np.pi * freq * time / period
    first = angle[:, :rows]
    forward = np.concatenate([np.cos(first), -np.sin(first)], axis=0)
    later = angle[:, rows:].T
    inverse = np.concatenate([np.cos(later), -np.sin(later)], axis=1) / rows
    return jnp.asarray(forward, jnp.bfloat16), jnp.asarray(inverse, jnp.bfloat16)


def room(mib, flops=0, moved=0):
    return dict(
        compiler_params=pltpu.CompilerParams(vmem_limit_bytes=mib * MIB),
        cost_estimate=pl.CostEstimate(flops=flops, bytes_accessed=moved, transcendentals=0),
    )


VMEM = pl.BlockSpec(memory_space=pltpu.VMEM)
SMEM = pl.BlockSpec(memory_space=pltpu.SMEM)
ANYWHERE = pl.BlockSpec(memory_space=pl.ANY)


def pack_kernel(*refs, count, parts):
    inputs, out, held, made, sems, out_sem = (
        refs[:count],
        refs[count],
        refs[count + 1 : 2 * count + 1],
        refs[-3],
        refs[-2],
        refs[-1],
    )
    size = inputs[0].shape[0] // parts
    copies = [
        [
            pltpu.make_async_copy(
                ref.at[pl.ds(s * size, size)], buf.at[pl.ds(s * size, size)], sems.at[i, s]
            )
            for i, (ref, buf) in enumerate(zip(inputs, held))
        ]
        for s in range(parts)
    ]
    for part in copies:
        for c in part:
            c.start()
    stores = []
    for s, part in enumerate(copies):
        span = slice(s * size, (s + 1) * size)
        for i, c in enumerate(part):
            c.wait()
            for p in range(out.shape[0]):
                lanes = slice(p * HEAD_DIM, (p + 1) * HEAD_DIM)
                made[p, i, span] = held[i][span, lanes].astype(jnp.bfloat16)
            rows = pl.ds(s * size, size)
            stores.append(
                pltpu.make_async_copy(made.at[:, i, rows], out.at[:, i, rows], out_sem.at[i, s])
            )
            stores[-1].start()
    for c in stores:
        c.wait()


def pack(*arrays):
    rows, channels = arrays[0].shape
    chips = channels // HEAD_DIM
    count = len(arrays)
    parts = 4
    shape = (chips, count, rows, HEAD_DIM)
    return pl.pallas_call(
        functools.partial(pack_kernel, count=count, parts=parts),
        in_specs=[ANYWHERE] * count,
        out_specs=ANYWHERE,
        out_shape=jax.ShapeDtypeStruct(shape, jnp.bfloat16),
        scratch_shapes=[pltpu.VMEM(a.shape, a.dtype) for a in arrays]
        + [pltpu.VMEM(shape, jnp.bfloat16)]
        + [pltpu.SemaphoreType.DMA((count, parts))] * 2,
        **room(24, 0, 6 * MIB),
    )(*[in_hbm(a) for a in arrays])


def pack_rest_kernel(queries, keys, forward, out, forward_out):
    for p in range(out.shape[0]):
        lanes = slice(p * HEAD_DIM, (p + 1) * HEAD_DIM)
        out[p, 0] = queries[:, lanes]
        out[p, 1] = keys[:, lanes]
    forward_out[...] = forward[...]


def pack_rest(queries, keys, forward):
    rows, channels = queries.shape
    shape = (channels // HEAD_DIM, 2, rows, HEAD_DIM)
    return pl.pallas_call(
        pack_rest_kernel,
        in_specs=[VMEM] * 3,
        out_specs=[VMEM] * 2,
        out_shape=[
            jax.ShapeDtypeStruct(shape, jnp.bfloat16),
            jax.ShapeDtypeStruct(forward.shape, jnp.bfloat16),
        ],
        **room(16, 0, 2 * MIB),
    )(queries, keys, forward)


def unpack_kernel(back, mixed, attended, sems):
    copies = []
    for p in range(back.shape[0]):
        lanes = pl.ds(p * HEAD_DIM, HEAD_DIM)
        for i, out in enumerate((mixed, attended)):
            copies.append(pltpu.make_async_copy(back.at[p, i], out.at[:, lanes], sems.at[i, p]))
    for c in copies:
        c.start()
    for c in copies:
        c.wait()


def unpack(back):
    chips, count, rows, lanes = back.shape
    out = jax.ShapeDtypeStruct((rows, chips * lanes), jnp.bfloat16)
    return pl.pallas_call(
        unpack_kernel,
        in_specs=[VMEM],
        out_specs=[ANYWHERE] * count,
        out_shape=[out] * count,
        scratch_shapes=[pltpu.SemaphoreType.DMA((count, chips))],
        **room(8, 0, 2 * MIB),
    )(back)


def conv_kernel(core_ref, own, x_other, h_any, skip_ref, forward, inverse_any, *refs):
    outs, refs = refs[:PARTS], refs[PARTS:]
    x_spec, h_spec, y_spec, made, h_other, inverse, tap_sem, table_sem, out_sem = refs
    blocks, _, rows, lanes = own.shape
    core = core_ref[0]
    copy = pltpu.make_async_copy
    half = blocks // PARTS
    taps = [
        copy(h_any.at[pl.ds(s * half, half)], h_other.at[pl.ds(s * half, half)], tap_sem.at[s])
        for s in range(PARTS)
    ]
    table = copy(inverse_any, inverse, table_sem.at[0])
    for c in taps + [table]:
        c.start()

    def dot(a, b):
        return jnp.dot(a, b, preferred_element_type=jnp.float32)

    h_spec[0] = jnp.zeros((2 * rows, lanes), jnp.float32)
    h_spec[1] = jnp.zeros((2 * rows, lanes), jnp.float32)
    for side in range(2):
        for m in range(blocks):
            if side == 1 and m % half == 0:
                taps[m // half].wait()
            pair = (x_other[m], h_other[m]) if side else (own[m, 0], own[m, 1])
            both = jnp.concatenate(pair, axis=1)
            spectrum = dot(forward[...], both)
            x_spec[2 * m + side] = spectrum[:, :lanes]
            at = 2 * m + 2 + (core if side == 0 else 1 - core)
            h_spec[at] = spectrum[:, lanes:]

    step = 8
    row = lax.broadcasted_iota(jnp.int32, (step, lanes), 0)
    sign = 1.0 - 2.0 * (row % 2).astype(jnp.float32)

    @pl.loop(0, rows // step)
    def _(t):
        re = pl.ds(pl.multiple_of(t * step, step), step)
        im = pl.ds(pl.multiple_of(rows + t * step, step), step)
        xr = [x_spec[j, re] for j in range(2 * blocks)]
        xi = [x_spec[j, im] for j in range(2 * blocks)]
        yr = [None] * blocks
        yi = [None] * blocks
        for lag in range(blocks):
            for side in range(2):
                k = 2 * lag + 1 if side == 0 else 2 * lag + 2 * core
                hr = h_spec[k, re] + sign * h_spec[k + 1, im]
                hi = h_spec[k, im] - sign * h_spec[k + 1, re]
                for j in range(blocks - lag):
                    b = j + lag
                    ar, ai = xr[2 * j + side], xi[2 * j + side]
                    pr = ar * hr - ai * hi
                    pi = ar * hi + ai * hr
                    yr[b] = pr if yr[b] is None else yr[b] + pr
                    yi[b] = pi if yi[b] is None else yi[b] + pi
        for b in range(blocks):
            y_spec[re, b * lanes : (b + 1) * lanes] = yr[b]
            y_spec[im, b * lanes : (b + 1) * lanes] = yi[b]

    table.wait()
    skip = skip_ref[...]
    stores = []
    for m in range(blocks // 2):
        spectrum = y_spec[:, 2 * m * lanes : 2 * (m + 1) * lanes]
        convolved = dot(inverse[...], spectrum.astype(jnp.bfloat16))
        for s in range(2):
            b = 2 * m + s
            part = convolved[:, s * lanes : (s + 1) * lanes]
            direct = skip * own[b, 0].astype(jnp.float32)
            made[b] = (own[b, 2].astype(jnp.float32) * (part + direct)).astype(jnp.bfloat16)
            stores.append(copy(made.at[b], outs[b // half].at[b % half], out_sem.at[b]))
            stores[-1].start()
    for c in stores:
        c.wait()


def in_hbm(array):
    return pltpu.with_memory_space_constraint(array, pltpu.HBM)


def convolve(core, own, x_other, h_other, skip, forward, inverse):
    blocks, _, rows, lanes = own.shape
    return pl.pallas_call(
        conv_kernel,
        in_specs=[SMEM, VMEM, VMEM, ANYWHERE, VMEM, VMEM, ANYWHERE],
        out_specs=[pl.BlockSpec(memory_space=pltpu.HBM)] * PARTS,
        out_shape=[jax.ShapeDtypeStruct((blocks // PARTS, rows, lanes), jnp.bfloat16)] * PARTS,
        scratch_shapes=[
            pltpu.VMEM((2 * blocks, 2 * rows, lanes), jnp.float32),
            pltpu.VMEM((2 * blocks + 2, 2 * rows, lanes), jnp.float32),
            pltpu.VMEM((2 * rows, blocks * lanes), jnp.float32),
            pltpu.VMEM((blocks, rows, lanes), jnp.bfloat16),
            pltpu.VMEM((blocks, rows, lanes), jnp.bfloat16),
            pltpu.VMEM(inverse.shape, jnp.bfloat16),
            pltpu.SemaphoreType.DMA((PARTS,)),
            pltpu.SemaphoreType.DMA((1,)),
            pltpu.SemaphoreType.DMA((blocks,)),
        ],
        **room(24, 10**6, MIB),
    )(core, own, x_other, in_hbm(h_other), skip, forward, in_hbm(inverse))


def attend_kernel(core_ref, qk_own, k_other, *refs):
    v_any, v_other, refs = refs[:PARTS], refs[PARTS : 2 * PARTS], refs[2 * PARTS :]
    out, v_own, v_sem = refs
    blocks, _, rows, lanes = qk_own.shape
    each = blocks // PARTS
    values = [
        pltpu.make_async_copy(part, v_own.at[pl.ds(i * each, each)], v_sem.at[i])
        for i, part in enumerate(v_any)
    ]
    for c in values:
        c.start()
    core = core_ref[0]
    row = lax.broadcasted_iota(jnp.int32, (rows, rows), 0)
    col = lax.broadcasted_iota(jnp.int32, (rows, rows), 1)
    on_diagonal = col <= row
    beside = jnp.full((rows, rows), core, jnp.int32) > 0
    ones = jnp.ones((rows, lanes), jnp.bfloat16)

    def product(q, k):
        return lax.dot_general(
            q, k, (((1,), (1,)), ((), ())), preferred_element_type=jnp.float32
        )

    def masked(b, j, s):
        if j == b:
            own = jnp.where(on_diagonal, s[:, :rows], MASKED)
            other = jnp.where(beside, s[:, rows:], MASKED)
            s = jnp.concatenate([own, other], axis=1)
        return s

    def scores(b, j):
        both = jnp.concatenate([qk_own[j, 1], k_other[j]], axis=0)
        return masked(b, j, product(qk_own[b, 0], both))

    order = list(range(blocks))[::-1]
    last = order[0]
    current = [scores(last, j) for j in range(blocks)]
    for c in values:
        c.wait()
    for i, b in enumerate(order):
        top = current[0]
        for s in current[1:]:
            top = jnp.maximum(top, s)
        top = jnp.max(top, axis=1, keepdims=True)
        later = order[i + 1] if i + 1 < blocks else -1
        following = []
        total = None
        for j in range(b + 1):
            if j <= later:
                following.append(scores(later, j))
            weights = jnp.exp2((current[j] - top) * TO_EXP2).astype(jnp.bfloat16)
            both = jnp.concatenate(
                [
                    jnp.concatenate([v_own[j], ones], axis=1),
                    jnp.concatenate([v_other[j // each][j % each], ones], axis=1),
                ],
                axis=0,
            )
            part = jnp.dot(weights, both, preferred_element_type=jnp.float32)
            total = part if total is None else total + part
        out[b, 0] = v_own[b]
        out[b, 1] = (total[:, :lanes] / total[:, lanes:]).astype(jnp.bfloat16)
        current = following


def attend(core, qk_own, k_other, v_own, v_other):
    blocks, _, rows, lanes = qk_own.shape
    return pl.pallas_call(
        attend_kernel,
        in_specs=[SMEM] + [VMEM] * 2 + [ANYWHERE] * PARTS + [VMEM] * PARTS,
        out_specs=VMEM,
        out_shape=jax.ShapeDtypeStruct((blocks, 2, rows, lanes), jnp.bfloat16),
        scratch_shapes=[
            pltpu.VMEM((blocks, rows, lanes), jnp.bfloat16),
            pltpu.SemaphoreType.DMA((PARTS,)),
        ],
        **room(24, 10**9, MIB),
    )(core, qk_own, k_other, *[in_hbm(v) for v in v_own], *v_other)


def to_chips(array):
    flat = array.reshape(array.shape[0], -1, array.shape[-1])
    moved = lax.all_to_all(flat, "chip", split_axis=0, concat_axis=0, tiled=True)
    return moved.reshape(array.shape)


def swap(array):
    return lax.ppermute(array, "core", [(0, 1), (1, 0)])


def per_device(gate_input, value_input, filter_taps, skip_gain, queries, keys):
    chip = lax.axis_index("chip")
    core = lax.axis_index("core").astype(jnp.int32).reshape(1)
    own = to_chips(pack(value_input, filter_taps, gate_input))
    forward, inverse = transform_tables(queries.shape[0])
    packed = pack_rest(queries, keys, forward)
    own, packed = lax.optimization_barrier((own, packed))
    qk_own = to_chips(packed[0])
    x_other, h_other = (swap(own[:, i]) for i in (0, 1))
    skip = lax.dynamic_slice(skip_gain, (chip * HEAD_DIM,), (HEAD_DIM,)).reshape(1, HEAD_DIM)
    v_own = convolve(core, own, x_other, h_other, skip, packed[1], inverse)
    qk_own, v_other = lax.optimization_barrier((qk_own, [swap(v) for v in v_own]))
    k_other = swap(qk_own[:, 1])
    back = to_chips(attend(core, qk_own, k_other, v_own, v_other))
    mixed, attended = unpack(back)
    return (mixed, attended)


def solution(mesh):
    ctx, tp = mesh.devices.shape
    fine = Mesh(mesh.devices.reshape(ctx // CORES, CORES, tp), ("chip", "core", "tp"))
    rows = P(("chip", "core"), "tp")
    return jax.shard_map(
        per_device,
        mesh=fine,
        in_specs=(rows, rows, rows, P("tp"), rows, rows),
        out_specs=(rows, rows),
        check_vma=False,
    )
```

```python
import functools
import math

import numpy as np

import jax
import jax.numpy as jnp
from jax import lax
from jax.experimental import pallas as pl
from jax.experimental.pallas import tpu as pltpu
from jax.sharding import Mesh, PartitionSpec as P

HEAD_DIM = 128
CORES = 2
SCALE = 1.0 / math.sqrt(HEAD_DIM)
MASKED = -1e30
PARTS = 2
TO_EXP2 = SCALE * math.log2(math.e)
MIB = 1024 * 1024


def transform_tables(rows):
    period = 2 * rows
    freq = np.arange(rows, dtype=np.float64)[:, None] + 0.5
    time = np.arange(period, dtype=np.float64)[None, :]
    angle = 2.0 * np.pi * freq * time / period
    first = angle[:, :rows]
    forward = np.concatenate([np.cos(first), -np.sin(first)], axis=0)
    later = angle[:, rows:].T
    inverse = np.concatenate([np.cos(later), -np.sin(later)], axis=1) / rows
    return jnp.asarray(forward, jnp.bfloat16), jnp.asarray(inverse, jnp.bfloat16)


def room(mib, flops=0, moved=0):
    return dict(
        compiler_params=pltpu.CompilerParams(vmem_limit_bytes=mib * MIB),
        cost_estimate=pl.CostEstimate(flops=flops, bytes_accessed=moved, transcendentals=0),
    )


VMEM = pl.BlockSpec(memory_space=pltpu.VMEM)
SMEM = pl.BlockSpec(memory_space=pltpu.SMEM)
ANYWHERE = pl.BlockSpec(memory_space=pl.ANY)


def pack_kernel(*refs, count, parts):
    inputs, out, held, made, sems, out_sem = (
        refs[:count],
        refs[count],
        refs[count + 1 : 2 * count + 1],
        refs[-3],
        refs[-2],
        refs[-1],
    )
    size = inputs[0].shape[0] // parts
    copies = [
        [
            pltpu.make_async_copy(
                ref.at[pl.ds(s * size, size)], buf.at[pl.ds(s * size, size)], sems.at[i, s]
            )
            for i, (ref, buf) in enumerate(zip(inputs, held))
        ]
        for s in range(parts)
    ]
    for part in copies:
        for c in part:
            c.start()
    stores = []
    for s, part in enumerate(copies):
        span = slice(s * size, (s + 1) * size)
        for i, c in enumerate(part):
            c.wait()
            for p in range(out.shape[0]):
                lanes = slice(p * HEAD_DIM, (p + 1) * HEAD_DIM)
                made[p, i, span] = held[i][span, lanes].astype(jnp.bfloat16)
            rows = pl.ds(s * size, size)
            stores.append(
                pltpu.make_async_copy(made.at[:, i, rows], out.at[:, i, rows], out_sem.at[i, s])
            )
            stores[-1].start()
    for c in stores:
        c.wait()


def pack(*arrays):
    rows, channels = arrays[0].shape
    chips = channels // HEAD_DIM
    count = len(arrays)
    parts = 4
    shape = (chips, count, rows, HEAD_DIM)
    return pl.pallas_call(
        functools.partial(pack_kernel, count=count, parts=parts),
        in_specs=[ANYWHERE] * count,
        out_specs=ANYWHERE,
        out_shape=jax.ShapeDtypeStruct(shape, jnp.bfloat16),
        scratch_shapes=[pltpu.VMEM(a.shape, a.dtype) for a in arrays]
        + [pltpu.VMEM(shape, jnp.bfloat16)]
        + [pltpu.SemaphoreType.DMA((count, parts))] * 2,
        **room(24, 0, 6 * MIB),
    )(*[in_hbm(a) for a in arrays])


def pack_rest_kernel(queries, keys, forward, out, forward_out):
    for p in range(out.shape[0]):
        lanes = slice(p * HEAD_DIM, (p + 1) * HEAD_DIM)
        out[p, 0] = queries[:, lanes]
        out[p, 1] = keys[:, lanes]
    forward_out[...] = forward[...]


def pack_rest(queries, keys, forward):
    rows, channels = queries.shape
    shape = (channels // HEAD_DIM, 2, rows, HEAD_DIM)
    return pl.pallas_call(
        pack_rest_kernel,
        in_specs=[VMEM] * 3,
        out_specs=[VMEM] * 2,
        out_shape=[
            jax.ShapeDtypeStruct(shape, jnp.bfloat16),
            jax.ShapeDtypeStruct(forward.shape, jnp.bfloat16),
        ],
        **room(16, 0, 2 * MIB),
    )(queries, keys, forward)


def unpack_kernel(back, mixed, attended, sems):
    copies = []
    for p in range(back.shape[0]):
        lanes = pl.ds(p * HEAD_DIM, HEAD_DIM)
        for i, out in enumerate((mixed, attended)):
            copies.append(pltpu.make_async_copy(back.at[p, i], out.at[:, lanes], sems.at[i, p]))
    for c in copies:
        c.start()
    for c in copies:
        c.wait()


def unpack(back):
    chips, count, rows, lanes = back.shape
    out = jax.ShapeDtypeStruct((rows, chips * lanes), jnp.bfloat16)
    return pl.pallas_call(
        unpack_kernel,
        in_specs=[VMEM],
        out_specs=[ANYWHERE] * count,
        out_shape=[out] * count,
        scratch_shapes=[pltpu.SemaphoreType.DMA((count, chips))],
        **room(8, 0, 2 * MIB),
    )(back)


def conv_kernel(core_ref, own, x_other, h_any, skip_ref, forward, inverse_any, *refs):
    outs, refs = refs[:PARTS], refs[PARTS:]
    x_spec, h_spec, y_spec, made, h_other, inverse, tap_sem, table_sem, out_sem = refs
    blocks, _, rows, lanes = own.shape
    core = core_ref[0]
    copy = pltpu.make_async_copy
    half = blocks // PARTS
    taps = [
        copy(h_any.at[pl.ds(s * half, half)], h_other.at[pl.ds(s * half, half)], tap_sem.at[s])
        for s in range(PARTS)
    ]
    table = copy(inverse_any, inverse, table_sem.at[0])
    for c in taps + [table]:
        c.start()

    def dot(a, b):
        return jnp.dot(a, b, preferred_element_type=jnp.float32)

    h_spec[0] = jnp.zeros((2 * rows, lanes), jnp.float32)
    h_spec[1] = jnp.zeros((2 * rows, lanes), jnp.float32)
    for side in range(2):
        for m in range(blocks):
            if side == 1 and m % half == 0:
                taps[m // half].wait()
            pair = (x_other[m], h_other[m]) if side else (own[m, 0], own[m, 1])
            both = jnp.concatenate(pair, axis=1)
            spectrum = dot(forward[...], both)
            x_spec[2 * m + side] = spectrum[:, :lanes]
            at = 2 * m + 2 + (core if side == 0 else 1 - core)
            h_spec[at] = spectrum[:, lanes:]

    step = 8
    row = lax.broadcasted_iota(jnp.int32, (step, lanes), 0)
    sign = 1.0 - 2.0 * (row % 2).astype(jnp.float32)

    @pl.loop(0, rows // step)
    def _(t):
        re = pl.ds(pl.multiple_of(t * step, step), step)
        im = pl.ds(pl.multiple_of(rows + t * step, step), step)
        xr = [x_spec[j, re] for j in range(2 * blocks)]
        xi = [x_spec[j, im] for j in range(2 * blocks)]
        yr = [None] * blocks
        yi = [None] * blocks
        for lag in range(blocks):
            for side in range(2):
                k = 2 * lag + 1 if side == 0 else 2 * lag + 2 * core
                hr = h_spec[k, re] + sign * h_spec[k + 1, im]
                hi = h_spec[k, im] - sign * h_spec[k + 1, re]
                for j in range(blocks - lag):
                    b = j + lag
                    ar, ai = xr[2 * j + side], xi[2 * j + side]
                    pr = ar * hr - ai * hi
                    pi = ar * hi + ai * hr
                    yr[b] = pr if yr[b] is None else yr[b] + pr
                    yi[b] = pi if yi[b] is None else yi[b] + pi
        for b in range(blocks):
            y_spec[re, b * lanes : (b + 1) * lanes] = yr[b]
            y_spec[im, b * lanes : (b + 1) * lanes] = yi[b]

    table.wait()
    skip = skip_ref[...]
    stores = []
    for m in range(blocks // 2):
        spectrum = y_spec[:, 2 * m * lanes : 2 * (m + 1) * lanes]
        convolved = dot(inverse[...], spectrum.astype(jnp.bfloat16))
        for s in range(2):
            b = 2 * m + s
            part = convolved[:, s * lanes : (s + 1) * lanes]
            direct = skip * own[b, 0].astype(jnp.float32)
            made[b] = (own[b, 2].astype(jnp.float32) * (part + direct)).astype(jnp.bfloat16)
            stores.append(copy(made.at[b], outs[b // half].at[b % half], out_sem.at[b]))
            stores[-1].start()
    for c in stores:
        c.wait()


def in_hbm(array):
    return pltpu.with_memory_space_constraint(array, pltpu.HBM)


def convolve(core, own, x_other, h_other, skip, forward, inverse):
    blocks, _, rows, lanes = own.shape
    return pl.pallas_call(
        conv_kernel,
        in_specs=[SMEM, VMEM, VMEM, ANYWHERE, VMEM, VMEM, ANYWHERE],
        out_specs=[pl.BlockSpec(memory_space=pltpu.HBM)] * PARTS,
        out_shape=[jax.ShapeDtypeStruct((blocks // PARTS, rows, lanes), jnp.bfloat16)] * PARTS,
        scratch_shapes=[
            pltpu.VMEM((2 * blocks, 2 * rows, lanes), jnp.float32),
            pltpu.VMEM((2 * blocks + 2, 2 * rows, lanes), jnp.float32),
            pltpu.VMEM((2 * rows, blocks * lanes), jnp.float32),
            pltpu.VMEM((blocks, rows, lanes), jnp.bfloat16),
            pltpu.VMEM((blocks, rows, lanes), jnp.bfloat16),
            pltpu.VMEM(inverse.shape, jnp.bfloat16),
            pltpu.SemaphoreType.DMA((PARTS,)),
            pltpu.SemaphoreType.DMA((1,)),
            pltpu.SemaphoreType.DMA((blocks,)),
        ],
        **room(24, 10**6, MIB),
    )(core, own, x_other, in_hbm(h_other), skip, forward, in_hbm(inverse))


def dot(a, b):
    return jnp.dot(a, b, preferred_element_type=jnp.float32)


def scores(q, k):
    return lax.dot_general(q, k, (((1,), (1,)), ((), ())), preferred_element_type=jnp.float32)


def chunks(count):
    return [(j, min(j + 2, count)) for j in range(0, count, 2)]


def rows_of(blocks, span):
    return jnp.concatenate([blocks[j][...] for j in range(*span)], axis=0)


def with_ones(values):
    return jnp.concatenate([values, jnp.ones(values.shape, values.dtype)], axis=1)


def sweep(blocks, make_scores, values, begin, finish):
    order = list(range(blocks))[::-1]
    current = [make_scores(order[0], span) for span in chunks(order[0] + 1)]
    for i, b in enumerate(order):
        top = current[0].max(axis=1, keepdims=True)
        for s in current[1:]:
            top = jnp.maximum(top, s.max(axis=1, keepdims=True))
        top, total = begin(b, top)
        later = chunks(order[i + 1] + 1) if i + 1 < blocks else []
        following = []
        for n, span in enumerate(chunks(b + 1)):
            if n < len(later):
                following.append(make_scores(order[i + 1], later[n]))
            s = current[n]
            wide = jnp.concatenate([top] * (s.shape[1] // top.shape[1]), axis=1)
            weights = jnp.exp2((s - wide) * TO_EXP2).astype(jnp.bfloat16)
            part = dot(weights, with_ones(rows_of(values, span)))
            total = part if total is None else total + part
        finish(b, top, total)
        current = following


def own_kernel(qk_own, *refs):
    v_any, refs = refs[:PARTS], refs[PARTS:]
    total_ref, top_ref, v_own, v_sem = refs
    blocks, _, rows, lanes = qk_own.shape
    each = blocks // PARTS
    loads = [
        pltpu.make_async_copy(part, v_own.at[pl.ds(i * each, each)], v_sem.at[i])
        for i, part in enumerate(v_any)
    ]
    for c in loads:
        c.start()
    row = lax.broadcasted_iota(jnp.int32, (rows, rows), 0)
    col = lax.broadcasted_iota(jnp.int32, (rows, rows), 1)
    on_diagonal = col <= row

    def make_scores(b, span):
        parts = []
        for j in range(*span):
            s = scores(qk_own[b, 0], qk_own[j, 1])
            parts.append(jnp.where(on_diagonal, s, MASKED) if j == b else s)
        return jnp.concatenate(parts, axis=1)

    def begin(b, top):
        if b == blocks - 1:
            for c in loads:
                c.wait()
        return jnp.broadcast_to(top, (rows, lanes)), None

    def finish(b, top, total):
        total_ref[b] = total
        top_ref[b] = top

    sweep(blocks, make_scores, [v_own.at[j] for j in range(blocks)], begin, finish)


def attend_own(qk_own, v_own):
    blocks, _, rows, lanes = qk_own.shape
    return pl.pallas_call(
        own_kernel,
        in_specs=[VMEM] + [ANYWHERE] * PARTS,
        out_specs=[VMEM] * 2,
        out_shape=[
            jax.ShapeDtypeStruct((blocks, rows, 2 * lanes), jnp.float32),
            jax.ShapeDtypeStruct((blocks, rows, lanes), jnp.float32),
        ],
        scratch_shapes=[
            pltpu.VMEM((blocks, rows, lanes), jnp.bfloat16),
            pltpu.SemaphoreType.DMA((PARTS,)),
        ],
        **room(24, 10**9, MIB),
    )(qk_own, *[in_hbm(v) for v in v_own])


def other_kernel(core_ref, qk_own, k_other, total_ref, top_ref, *refs):
    v_any, v_other, refs = refs[:PARTS], refs[PARTS : 2 * PARTS], refs[2 * PARTS :]
    out, v_sem = refs
    blocks, _, rows, lanes = qk_own.shape
    each = blocks // PARTS
    stores = [
        pltpu.make_async_copy(part, out.at[pl.ds(i * each, each), 0], v_sem.at[i])
        for i, part in enumerate(v_any)
    ]
    for c in stores:
        c.start()
    beside = jnp.full((rows, rows), core_ref[0], jnp.int32) > 0

    def make_scores(b, span):
        parts = []
        for j in range(*span):
            s = scores(qk_own[b, 0], k_other[j])
            parts.append(jnp.where(beside, s, MASKED) if j == b else s)
        return jnp.concatenate(parts, axis=1)

    def begin(b, top):
        before = top_ref[b]
        top = jnp.maximum(before, top)
        shrink = jnp.exp2((before - top) * TO_EXP2)
        return top, total_ref[b] * jnp.concatenate([shrink, shrink], axis=1)

    def finish(b, top, total):
        out[b, 1] = (total[:, :lanes] / total[:, lanes:]).astype(jnp.bfloat16)

    values = [v_other[j // each].at[j % each] for j in range(blocks)]
    sweep(blocks, make_scores, values, begin, finish)
    for c in stores:
        c.wait()


def attend_other(core, qk_own, k_other, total, top, v_own, v_other):
    blocks, _, rows, lanes = qk_own.shape
    return pl.pallas_call(
        other_kernel,
        in_specs=[SMEM] + [VMEM] * 4 + [ANYWHERE] * PARTS + [VMEM] * PARTS,
        out_specs=VMEM,
        out_shape=jax.ShapeDtypeStruct((blocks, 2, rows, lanes), jnp.bfloat16),
        scratch_shapes=[pltpu.SemaphoreType.DMA((PARTS,))],
        **room(24, 10**9, MIB),
    )(core, qk_own, k_other, total, top, *[in_hbm(v) for v in v_own], *v_other)


def to_chips(array):
    flat = array.reshape(array.shape[0], -1, array.shape[-1])
    moved = lax.all_to_all(flat, "chip", split_axis=0, concat_axis=0, tiled=True)
    return moved.reshape(array.shape)


def swap(array):
    return lax.ppermute(array, "core", [(0, 1), (1, 0)])


def per_device(gate_input, value_input, filter_taps, skip_gain, queries, keys):
    chip = lax.axis_index("chip")
    core = lax.axis_index("core").astype(jnp.int32).reshape(1)
    own = to_chips(pack(value_input, filter_taps, gate_input))
    forward, inverse = transform_tables(queries.shape[0])
    packed = pack_rest(queries, keys, forward)
    own, packed = lax.optimization_barrier((own, packed))
    qk_own = to_chips(packed[0])
    x_other, h_other = (swap(own[:, i]) for i in (0, 1))
    skip = lax.dynamic_slice(skip_gain, (chip * HEAD_DIM,), (HEAD_DIM,)).reshape(1, HEAD_DIM)
    v_own = convolve(core, own, x_other, h_other, skip, packed[1], inverse)
    qk_own, v_other = lax.optimization_barrier((qk_own, [swap(v) for v in v_own]))
    k_other = swap(qk_own[:, 1])
    total, top = attend_own(qk_own, v_own)
    back = to_chips(attend_other(core, qk_own, k_other, total, top, v_own, v_other))
    mixed, attended = unpack(back)
    return (mixed, attended)


def solution(mesh):
    ctx, tp = mesh.devices.shape
    fine = Mesh(mesh.devices.reshape(ctx // CORES, CORES, tp), ("chip", "core", "tp"))
    rows = P(("chip", "core"), "tp")
    return jax.shard_map(
        per_device,
        mesh=fine,
        in_specs=(rows, rows, rows, P("tp"), rows, rows),
        out_specs=(rows, rows),
        check_vma=False,
    )
```

```python
import functools
import math

import numpy as np

import jax
import jax.numpy as jnp
from jax import lax
from jax.experimental import pallas as pl
from jax.experimental.pallas import tpu as pltpu
from jax.sharding import Mesh, PartitionSpec as P

HEAD_DIM = 128
CORES = 2
SCALE = 1.0 / math.sqrt(HEAD_DIM)
MASKED = -1e30
PARTS = 2
TO_EXP2 = SCALE * math.log2(math.e)
MIB = 1024 * 1024


def transform_tables(rows):
    period = 2 * rows
    freq = np.arange(rows, dtype=np.float64)[:, None] + 0.5
    time = np.arange(period, dtype=np.float64)[None, :]
    angle = 2.0 * np.pi * freq * time / period
    first = angle[:, :rows]
    forward = np.concatenate([np.cos(first), -np.sin(first)], axis=0)
    later = angle[:, rows:].T
    inverse = np.concatenate([np.cos(later), -np.sin(later)], axis=1) / rows
    return jnp.asarray(forward, jnp.bfloat16), jnp.asarray(inverse, jnp.bfloat16)


def room(mib, flops=0, moved=0):
    return dict(
        compiler_params=pltpu.CompilerParams(vmem_limit_bytes=mib * MIB),
        cost_estimate=pl.CostEstimate(flops=flops, bytes_accessed=moved, transcendentals=0),
    )


VMEM = pl.BlockSpec(memory_space=pltpu.VMEM)
SMEM = pl.BlockSpec(memory_space=pltpu.SMEM)
ANYWHERE = pl.BlockSpec(memory_space=pl.ANY)


def pack_kernel(*refs, count, parts):
    inputs, out, held, made, sems, out_sem = (
        refs[:count],
        refs[count],
        refs[count + 1 : 2 * count + 1],
        refs[-3],
        refs[-2],
        refs[-1],
    )
    size = inputs[0].shape[0] // parts
    copies = [
        [
            pltpu.make_async_copy(
                ref.at[pl.ds(s * size, size)], buf.at[pl.ds(s * size, size)], sems.at[i, s]
            )
            for i, (ref, buf) in enumerate(zip(inputs, held))
        ]
        for s in range(parts)
    ]
    for part in copies:
        for c in part:
            c.start()
    stores = []
    for s, part in enumerate(copies):
        span = slice(s * size, (s + 1) * size)
        for i, c in enumerate(part):
            c.wait()
            for p in range(out.shape[0]):
                lanes = slice(p * HEAD_DIM, (p + 1) * HEAD_DIM)
                made[p, i, span] = held[i][span, lanes].astype(jnp.bfloat16)
            rows = pl.ds(s * size, size)
            stores.append(
                pltpu.make_async_copy(made.at[:, i, rows], out.at[:, i, rows], out_sem.at[i, s])
            )
            stores[-1].start()
    for c in stores:
        c.wait()


def pack(*arrays):
    rows, channels = arrays[0].shape
    chips = channels // HEAD_DIM
    count = len(arrays)
    parts = 2
    shape = (chips, count, rows, HEAD_DIM)
    return pl.pallas_call(
        functools.partial(pack_kernel, count=count, parts=parts),
        in_specs=[ANYWHERE] * count,
        out_specs=ANYWHERE,
        out_shape=jax.ShapeDtypeStruct(shape, jnp.bfloat16),
        scratch_shapes=[pltpu.VMEM(a.shape, a.dtype) for a in arrays]
        + [pltpu.VMEM(shape, jnp.bfloat16)]
        + [pltpu.SemaphoreType.DMA((count, parts))] * 2,
        **room(24, 0, 6 * MIB),
    )(*[in_hbm(a) for a in arrays])


def pack_rest_kernel(queries, keys, forward, out, forward_out):
    for p in range(out.shape[0]):
        lanes = slice(p * HEAD_DIM, (p + 1) * HEAD_DIM)
        out[p, 0] = queries[:, lanes]
        out[p, 1] = keys[:, lanes]
    forward_out[...] = forward[...]


def pack_rest(queries, keys, forward):
    rows, channels = queries.shape
    shape = (channels // HEAD_DIM, 2, rows, HEAD_DIM)
    return pl.pallas_call(
        pack_rest_kernel,
        in_specs=[VMEM] * 3,
        out_specs=[VMEM] * 2,
        out_shape=[
            jax.ShapeDtypeStruct(shape, jnp.bfloat16),
            jax.ShapeDtypeStruct(forward.shape, jnp.bfloat16),
        ],
        **room(16, 0, 2 * MIB),
    )(queries, keys, forward)


def unpack_kernel(back, mixed, attended, sems):
    copies = []
    for p in range(back.shape[0]):
        lanes = pl.ds(p * HEAD_DIM, HEAD_DIM)
        for i, out in enumerate((mixed, attended)):
            copies.append(pltpu.make_async_copy(back.at[p, i], out.at[:, lanes], sems.at[i, p]))
    for c in copies:
        c.start()
    for c in copies:
        c.wait()


def unpack(back):
    chips, count, rows, lanes = back.shape
    out = jax.ShapeDtypeStruct((rows, chips * lanes), jnp.bfloat16)
    return pl.pallas_call(
        unpack_kernel,
        in_specs=[VMEM],
        out_specs=[ANYWHERE] * count,
        out_shape=[out] * count,
        scratch_shapes=[pltpu.SemaphoreType.DMA((count, chips))],
        **room(8, 0, 2 * MIB),
    )(back)


def conv_kernel(core_ref, own, x_other, h_any, skip_ref, forward, inverse_any, *refs):
    outs, refs = refs[:PARTS], refs[PARTS:]
    x_spec, h_spec, y_spec, made, h_other, inverse, tap_sem, table_sem, out_sem = refs
    blocks, _, rows, lanes = own.shape
    core = core_ref[0]
    copy = pltpu.make_async_copy
    half = blocks // PARTS
    taps = [
        copy(h_any.at[pl.ds(s * half, half)], h_other.at[pl.ds(s * half, half)], tap_sem.at[s])
        for s in range(PARTS)
    ]
    table = copy(inverse_any, inverse, table_sem.at[0])
    for c in taps + [table]:
        c.start()

    def dot(a, b):
        return jnp.dot(a, b, preferred_element_type=jnp.float32)

    h_spec[0] = jnp.zeros((2 * rows, lanes), jnp.float32)
    h_spec[1] = jnp.zeros((2 * rows, lanes), jnp.float32)
    for side in range(2):
        for m in range(blocks):
            if side == 1 and m % half == 0:
                taps[m // half].wait()
            pair = (x_other[m], h_other[m]) if side else (own[m, 0], own[m, 1])
            both = jnp.concatenate(pair, axis=1)
            spectrum = dot(forward[...], both)
            x_spec[2 * m + side] = spectrum[:, :lanes]
            at = 2 * m + 2 + (core if side == 0 else 1 - core)
            h_spec[at] = spectrum[:, lanes:]

    step = 8
    row = lax.broadcasted_iota(jnp.int32, (step, lanes), 0)
    sign = 1.0 - 2.0 * (row % 2).astype(jnp.float32)

    @pl.loop(0, rows // step)
    def _(t):
        re = pl.ds(pl.multiple_of(t * step, step), step)
        im = pl.ds(pl.multiple_of(rows + t * step, step), step)
        xr = [x_spec[j, re] for j in range(2 * blocks)]
        xi = [x_spec[j, im] for j in range(2 * blocks)]
        yr = [None] * blocks
        yi = [None] * blocks
        for lag in range(blocks):
            for side in range(2):
                k = 2 * lag + 1 if side == 0 else 2 * lag + 2 * core
                hr = h_spec[k, re] + sign * h_spec[k + 1, im]
                hi = h_spec[k, im] - sign * h_spec[k + 1, re]
                for j in range(blocks - lag):
                    b = j + lag
                    ar, ai = xr[2 * j + side], xi[2 * j + side]
                    pr = ar * hr - ai * hi
                    pi = ar * hi + ai * hr
                    yr[b] = pr if yr[b] is None else yr[b] + pr
                    yi[b] = pi if yi[b] is None else yi[b] + pi
        for b in range(blocks):
            y_spec[re, b * lanes : (b + 1) * lanes] = yr[b]
            y_spec[im, b * lanes : (b + 1) * lanes] = yi[b]

    table.wait()
    skip = skip_ref[...]
    stores = []
    for m in range(blocks // 2):
        spectrum = y_spec[:, 2 * m * lanes : 2 * (m + 1) * lanes]
        convolved = dot(inverse[...], spectrum.astype(jnp.bfloat16))
        for s in range(2):
            b = 2 * m + s
            part = convolved[:, s * lanes : (s + 1) * lanes]
            direct = skip * own[b, 0].astype(jnp.float32)
            made[b] = (own[b, 2].astype(jnp.float32) * (part + direct)).astype(jnp.bfloat16)
            stores.append(copy(made.at[b], outs[b // half].at[b % half], out_sem.at[b]))
            stores[-1].start()
    for c in stores:
        c.wait()


def in_hbm(array):
    return pltpu.with_memory_space_constraint(array, pltpu.HBM)


def convolve(core, own, x_other, h_other, skip, forward, inverse):
    blocks, _, rows, lanes = own.shape
    return pl.pallas_call(
        conv_kernel,
        in_specs=[SMEM, VMEM, VMEM, ANYWHERE, VMEM, VMEM, ANYWHERE],
        out_specs=[pl.BlockSpec(memory_space=pltpu.HBM)] * PARTS,
        out_shape=[jax.ShapeDtypeStruct((blocks // PARTS, rows, lanes), jnp.bfloat16)] * PARTS,
        scratch_shapes=[
            pltpu.VMEM((2 * blocks, 2 * rows, lanes), jnp.float32),
            pltpu.VMEM((2 * blocks + 2, 2 * rows, lanes), jnp.float32),
            pltpu.VMEM((2 * rows, blocks * lanes), jnp.float32),
            pltpu.VMEM((blocks, rows, lanes), jnp.bfloat16),
            pltpu.VMEM((blocks, rows, lanes), jnp.bfloat16),
            pltpu.VMEM(inverse.shape, jnp.bfloat16),
            pltpu.SemaphoreType.DMA((PARTS,)),
            pltpu.SemaphoreType.DMA((1,)),
            pltpu.SemaphoreType.DMA((blocks,)),
        ],
        **room(24, 10**6, MIB),
    )(core, own, x_other, in_hbm(h_other), skip, forward, in_hbm(inverse))


def dot(a, b):
    return jnp.dot(a, b, preferred_element_type=jnp.float32)


def scores(q, k):
    return lax.dot_general(q, k, (((1,), (1,)), ((), ())), preferred_element_type=jnp.float32)


def chunks(count):
    return [(j, min(j + 2, count)) for j in range(0, count, 2)]


def rows_of(blocks, span):
    return jnp.concatenate([blocks[j][...] for j in range(*span)], axis=0)


def with_ones(values):
    return jnp.concatenate([values, jnp.ones(values.shape, values.dtype)], axis=1)


def sweep(blocks, make_scores, values, begin, finish, ahead=0):
    order = list(range(blocks))[::-1]
    current = [make_scores(order[0], span) for span in chunks(order[0] + 1)]
    early = [make_scores(b, span) for b in order[1 : 1 + ahead] for span in chunks(b + 1)]
    for i, b in enumerate(order):
        top = current[0].max(axis=1, keepdims=True)
        for s in current[1:]:
            top = jnp.maximum(top, s.max(axis=1, keepdims=True))
        top, total = begin(b, top)
        later = chunks(order[i + 1] + 1) if i + 1 < blocks else []
        following = early[: len(later)] if i < ahead else []
        early = early[len(later) :] if i < ahead else []
        later = [] if i < ahead else later
        for n, span in enumerate(chunks(b + 1)):
            if n < len(later):
                following.append(make_scores(order[i + 1], later[n]))
            s = current[n]
            wide = jnp.concatenate([top] * (s.shape[1] // top.shape[1]), axis=1)
            weights = jnp.exp2((s - wide) * TO_EXP2).astype(jnp.bfloat16)
            part = dot(weights, with_ones(rows_of(values, span)))
            total = part if total is None else total + part
        finish(b, top, total)
        current = following


def own_kernel(qk_own, *refs):
    v_any, refs = refs[:PARTS], refs[PARTS:]
    total_ref, top_ref, v_own, v_sem = refs
    blocks, _, rows, lanes = qk_own.shape
    each = blocks // PARTS
    loads = [
        pltpu.make_async_copy(part, v_own.at[pl.ds(i * each, each)], v_sem.at[i])
        for i, part in enumerate(v_any)
    ]
    for c in loads:
        c.start()
    row = lax.broadcasted_iota(jnp.int32, (rows, rows), 0)
    col = lax.broadcasted_iota(jnp.int32, (rows, rows), 1)
    on_diagonal = col <= row

    def make_scores(b, span):
        parts = []
        for j in range(*span):
            s = scores(qk_own[b, 0], qk_own[j, 1])
            parts.append(jnp.where(on_diagonal, s, MASKED) if j == b else s)
        return jnp.concatenate(parts, axis=1)

    def begin(b, top):
        if b == blocks - 1:
            for c in loads:
                c.wait()
        return jnp.broadcast_to(top, (rows, lanes)), None

    def finish(b, top, total):
        total_ref[b] = total
        top_ref[b] = top

    sweep(blocks, make_scores, [v_own.at[j] for j in range(blocks)], begin, finish, 1)


def attend_own(qk_own, v_own):
    blocks, _, rows, lanes = qk_own.shape
    return pl.pallas_call(
        own_kernel,
        in_specs=[VMEM] + [ANYWHERE] * PARTS,
        out_specs=[VMEM] * 2,
        out_shape=[
            jax.ShapeDtypeStruct((blocks, rows, 2 * lanes), jnp.float32),
            jax.ShapeDtypeStruct((blocks, rows, lanes), jnp.float32),
        ],
        scratch_shapes=[
            pltpu.VMEM((blocks, rows, lanes), jnp.bfloat16),
            pltpu.SemaphoreType.DMA((PARTS,)),
        ],
        **room(24, 10**9, MIB),
    )(qk_own, *[in_hbm(v) for v in v_own])


def other_kernel(core_ref, qk_own, k_other, total_ref, top_ref, *refs):
    v_any, v_other, refs = refs[:PARTS], refs[PARTS : 2 * PARTS], refs[2 * PARTS :]
    out, v_sem = refs
    blocks, _, rows, lanes = qk_own.shape
    each = blocks // PARTS
    stores = [
        pltpu.make_async_copy(part, out.at[pl.ds(i * each, each), 0], v_sem.at[i])
        for i, part in enumerate(v_any)
    ]
    for c in stores:
        c.start()
    beside = jnp.full((rows, rows), core_ref[0], jnp.int32) > 0

    def make_scores(b, span):
        parts = []
        for j in range(*span):
            s = scores(qk_own[b, 0], k_other[j])
            parts.append(jnp.where(beside, s, MASKED) if j == b else s)
        return jnp.concatenate(parts, axis=1)

    def begin(b, top):
        before = top_ref[b]
        top = jnp.maximum(before, top)
        shrink = jnp.exp2((before - top) * TO_EXP2)
        return top, total_ref[b] * jnp.concatenate([shrink, shrink], axis=1)

    def finish(b, top, total):
        out[b, 1] = (total[:, :lanes] / total[:, lanes:]).astype(jnp.bfloat16)

    values = [v_other[j // each].at[j % each] for j in range(blocks)]
    sweep(blocks, make_scores, values, begin, finish)
    for c in stores:
        c.wait()


def attend_other(core, qk_own, k_other, total, top, v_own, v_other):
    blocks, _, rows, lanes = qk_own.shape
    return pl.pallas_call(
        other_kernel,
        in_specs=[SMEM] + [VMEM] * 4 + [ANYWHERE] * PARTS + [VMEM] * PARTS,
        out_specs=VMEM,
        out_shape=jax.ShapeDtypeStruct((blocks, 2, rows, lanes), jnp.bfloat16),
        scratch_shapes=[pltpu.SemaphoreType.DMA((PARTS,))],
        **room(24, 10**9, MIB),
    )(core, qk_own, k_other, total, top, *[in_hbm(v) for v in v_own], *v_other)


def to_chips(array):
    flat = array.reshape(array.shape[0], -1, array.shape[-1])
    moved = lax.all_to_all(flat, "chip", split_axis=0, concat_axis=0, tiled=True)
    return moved.reshape(array.shape)


def swap(array):
    return lax.ppermute(array, "core", [(0, 1), (1, 0)])


def per_device(gate_input, value_input, filter_taps, skip_gain, queries, keys):
    chip = lax.axis_index("chip")
    core = lax.axis_index("core").astype(jnp.int32).reshape(1)
    own = to_chips(pack(value_input, filter_taps, gate_input))
    forward, inverse = transform_tables(queries.shape[0])
    packed = pack_rest(queries, keys, forward)
    own, packed = lax.optimization_barrier((own, packed))
    qk_own = to_chips(packed[0])
    x_other, h_other = (swap(own[:, i]) for i in (0, 1))
    skip = lax.dynamic_slice(skip_gain, (chip * HEAD_DIM,), (HEAD_DIM,)).reshape(1, HEAD_DIM)
    v_own = convolve(core, own, x_other, h_other, skip, packed[1], inverse)
    qk_own, v_other = lax.optimization_barrier((qk_own, [swap(v) for v in v_own]))
    k_other = swap(qk_own[:, 1])
    total, top = attend_own(qk_own, v_own)
    back = to_chips(attend_other(core, qk_own, k_other, total, top, v_own, v_other))
    mixed, attended = unpack(back)
    return (mixed, attended)


def solution(mesh):
    ctx, tp = mesh.devices.shape
    fine = Mesh(mesh.devices.reshape(ctx // CORES, CORES, tp), ("chip", "core", "tp"))
    rows = P(("chip", "core"), "tp")
    return jax.shard_map(
        per_device,
        mesh=fine,
        in_specs=(rows, rows, rows, P("tp"), rows, rows),
        out_specs=(rows, rows),
        check_vma=False,
    )
```

```python
import functools
import math

import numpy as np

import jax
import jax.numpy as jnp
from jax import lax
from jax.experimental import pallas as pl
from jax.experimental.pallas import tpu as pltpu
from jax.sharding import Mesh, PartitionSpec as P

HEAD_DIM = 128
CORES = 2
SCALE = 1.0 / math.sqrt(HEAD_DIM)
MASKED = -1e30
PARTS = 2
TO_EXP2 = SCALE * math.log2(math.e)
MIB = 1024 * 1024


def transform_tables(rows):
    period = 2 * rows
    freq = np.arange(rows, dtype=np.float64)[:, None] + 0.5
    time = np.arange(period, dtype=np.float64)[None, :]
    angle = 2.0 * np.pi * freq * time / period
    first = angle[:, :rows]
    forward = np.concatenate([np.cos(first), -np.sin(first)], axis=0)
    later = angle[:, rows:].T
    inverse = np.concatenate([np.cos(later), -np.sin(later)], axis=1) / rows
    return jnp.asarray(forward, jnp.bfloat16), jnp.asarray(inverse, jnp.bfloat16)


def room(mib, flops=0, moved=0):
    return dict(
        compiler_params=pltpu.CompilerParams(vmem_limit_bytes=mib * MIB),
        cost_estimate=pl.CostEstimate(flops=flops, bytes_accessed=moved, transcendentals=0),
    )


VMEM = pl.BlockSpec(memory_space=pltpu.VMEM)
SMEM = pl.BlockSpec(memory_space=pltpu.SMEM)
ANYWHERE = pl.BlockSpec(memory_space=pl.ANY)


def pack_kernel(*refs, count, parts):
    inputs, out, held, made, sems, out_sem = (
        refs[:count],
        refs[count],
        refs[count + 1 : 2 * count + 1],
        refs[-3],
        refs[-2],
        refs[-1],
    )
    size = inputs[0].shape[0] // parts
    copies = [
        [
            pltpu.make_async_copy(
                ref.at[pl.ds(s * size, size)], buf.at[pl.ds(s * size, size)], sems.at[i, s]
            )
            for i, (ref, buf) in enumerate(zip(inputs, held))
        ]
        for s in range(parts)
    ]
    for part in copies:
        for c in part:
            c.start()
    stores = []
    for s, part in enumerate(copies):
        span = slice(s * size, (s + 1) * size)
        for i, c in enumerate(part):
            c.wait()
            for p in range(out.shape[0]):
                lanes = slice(p * HEAD_DIM, (p + 1) * HEAD_DIM)
                made[p, i, span] = held[i][span, lanes].astype(jnp.bfloat16)
            rows = pl.ds(s * size, size)
            stores.append(
                pltpu.make_async_copy(made.at[:, i, rows], out.at[:, i, rows], out_sem.at[i, s])
            )
            stores[-1].start()
    for c in stores:
        c.wait()


def pack(*arrays):
    rows, channels = arrays[0].shape
    chips = channels // HEAD_DIM
    count = len(arrays)
    parts = 2
    shape = (chips, count, rows, HEAD_DIM)
    return pl.pallas_call(
        functools.partial(pack_kernel, count=count, parts=parts),
        in_specs=[ANYWHERE] * count,
        out_specs=ANYWHERE,
        out_shape=jax.ShapeDtypeStruct(shape, jnp.bfloat16),
        scratch_shapes=[pltpu.VMEM(a.shape, a.dtype) for a in arrays]
        + [pltpu.VMEM(shape, jnp.bfloat16)]
        + [pltpu.SemaphoreType.DMA((count, parts))] * 2,
        **room(24, 0, 6 * MIB),
    )(*[in_hbm(a) for a in arrays])


def pack_rest_kernel(queries, keys, forward, out, forward_out):
    for p in range(out.shape[0]):
        lanes = slice(p * HEAD_DIM, (p + 1) * HEAD_DIM)
        out[p, 0] = queries[:, lanes]
        out[p, 1] = keys[:, lanes]
    forward_out[...] = forward[...]


def pack_rest(queries, keys, forward):
    rows, channels = queries.shape
    shape = (channels // HEAD_DIM, 2, rows, HEAD_DIM)
    return pl.pallas_call(
        pack_rest_kernel,
        in_specs=[VMEM] * 3,
        out_specs=[VMEM] * 2,
        out_shape=[
            jax.ShapeDtypeStruct(shape, jnp.bfloat16),
            jax.ShapeDtypeStruct(forward.shape, jnp.bfloat16),
        ],
        **room(16, 0, 2 * MIB),
    )(queries, keys, forward)


def unpack_kernel(back, mixed, attended, sems):
    copies = []
    for p in range(back.shape[0]):
        lanes = pl.ds(p * HEAD_DIM, HEAD_DIM)
        for i, out in enumerate((mixed, attended)):
            copies.append(pltpu.make_async_copy(back.at[p, i], out.at[:, lanes], sems.at[i, p]))
    for c in copies:
        c.start()
    for c in copies:
        c.wait()


def unpack(back):
    chips, count, rows, lanes = back.shape
    out = jax.ShapeDtypeStruct((rows, chips * lanes), jnp.bfloat16)
    return pl.pallas_call(
        unpack_kernel,
        in_specs=[VMEM],
        out_specs=[ANYWHERE] * count,
        out_shape=[out] * count,
        scratch_shapes=[pltpu.SemaphoreType.DMA((count, chips))],
        **room(8, 0, 2 * MIB),
    )(back)


def conv_kernel(core_ref, own, x_other, h_any, skip_ref, forward, inverse_any, *refs):
    outs, refs = refs[:PARTS], refs[PARTS:]
    x_spec, h_spec, y_spec, made, h_other, inverse, tap_sem, table_sem, out_sem = refs
    blocks, _, rows, lanes = own.shape
    core = core_ref[0]
    copy = pltpu.make_async_copy
    half = blocks // PARTS
    taps = [
        copy(h_any.at[pl.ds(s * half, half)], h_other.at[pl.ds(s * half, half)], tap_sem.at[s])
        for s in range(PARTS)
    ]
    table = copy(inverse_any, inverse, table_sem.at[0])
    for c in taps + [table]:
        c.start()

    def dot(a, b):
        return jnp.dot(a, b, preferred_element_type=jnp.float32)

    h_spec[0] = jnp.zeros((2 * rows, lanes), jnp.float32)
    h_spec[1] = jnp.zeros((2 * rows, lanes), jnp.float32)
    for side in range(2):
        for m in range(blocks):
            if side == 1 and m % half == 0:
                taps[m // half].wait()
            pair = (x_other[m], h_other[m]) if side else (own[m, 0], own[m, 1])
            both = jnp.concatenate(pair, axis=1)
            spectrum = dot(forward[...], both)
            x_spec[2 * m + side] = spectrum[:, :lanes]
            at = 2 * m + 2 + (core if side == 0 else 1 - core)
            h_spec[at] = spectrum[:, lanes:]

    step = 8
    row = lax.broadcasted_iota(jnp.int32, (step, lanes), 0)
    sign = 1.0 - 2.0 * (row % 2).astype(jnp.float32)

    @pl.loop(0, rows // step)
    def _(t):
        re = pl.ds(pl.multiple_of(t * step, step), step)
        im = pl.ds(pl.multiple_of(rows + t * step, step), step)
        xr = [x_spec[j, re] for j in range(2 * blocks)]
        xi = [x_spec[j, im] for j in range(2 * blocks)]
        yr = [None] * blocks
        yi = [None] * blocks
        for lag in range(blocks):
            for side in range(2):
                k = 2 * lag + 1 if side == 0 else 2 * lag + 2 * core
                hr = h_spec[k, re] + sign * h_spec[k + 1, im]
                hi = h_spec[k, im] - sign * h_spec[k + 1, re]
                for j in range(blocks - lag):
                    b = j + lag
                    ar, ai = xr[2 * j + side], xi[2 * j + side]
                    pr = ar * hr - ai * hi
                    pi = ar * hi + ai * hr
                    yr[b] = pr if yr[b] is None else yr[b] + pr
                    yi[b] = pi if yi[b] is None else yi[b] + pi
        for b in range(blocks):
            y_spec[re, b * lanes : (b + 1) * lanes] = yr[b]
            y_spec[im, b * lanes : (b + 1) * lanes] = yi[b]

    table.wait()
    skip = skip_ref[...]
    stores = []
    for m in range(blocks // 2):
        spectrum = y_spec[:, 2 * m * lanes : 2 * (m + 1) * lanes]
        convolved = dot(inverse[...], spectrum.astype(jnp.bfloat16))
        for s in range(2):
            b = 2 * m + s
            part = convolved[:, s * lanes : (s + 1) * lanes]
            direct = skip * own[b, 0].astype(jnp.float32)
            made[b] = (own[b, 2].astype(jnp.float32) * (part + direct)).astype(jnp.bfloat16)
            stores.append(copy(made.at[b], outs[b // half].at[b % half], out_sem.at[b]))
            stores[-1].start()
    for c in stores:
        c.wait()


def in_hbm(array):
    return pltpu.with_memory_space_constraint(array, pltpu.HBM)


def convolve(core, own, x_other, h_other, skip, forward, inverse):
    blocks, _, rows, lanes = own.shape
    return pl.pallas_call(
        conv_kernel,
        in_specs=[SMEM, VMEM, VMEM, ANYWHERE, VMEM, VMEM, ANYWHERE],
        out_specs=[pl.BlockSpec(memory_space=pltpu.HBM)] * PARTS,
        out_shape=[jax.ShapeDtypeStruct((blocks // PARTS, rows, lanes), jnp.bfloat16)] * PARTS,
        scratch_shapes=[
            pltpu.VMEM((2 * blocks, 2 * rows, lanes), jnp.float32),
            pltpu.VMEM((2 * blocks + 2, 2 * rows, lanes), jnp.float32),
            pltpu.VMEM((2 * rows, blocks * lanes), jnp.float32),
            pltpu.VMEM((blocks, rows, lanes), jnp.bfloat16),
            pltpu.VMEM((blocks, rows, lanes), jnp.bfloat16),
            pltpu.VMEM(inverse.shape, jnp.bfloat16),
            pltpu.SemaphoreType.DMA((PARTS,)),
            pltpu.SemaphoreType.DMA((1,)),
            pltpu.SemaphoreType.DMA((blocks,)),
        ],
        **room(24, 10**6, MIB),
    )(core, own, x_other, in_hbm(h_other), skip, forward, in_hbm(inverse))


def dot(a, b):
    return jnp.dot(a, b, preferred_element_type=jnp.float32)


def scores(q, k):
    return lax.dot_general(q, k, (((1,), (1,)), ((), ())), preferred_element_type=jnp.float32)


def chunks(count):
    return [(j, min(j + 2, count)) for j in range(0, count, 2)]


def rows_of(blocks, span):
    return jnp.concatenate([blocks[j][...] for j in range(*span)], axis=0)


def with_ones(values):
    return jnp.concatenate([values, jnp.ones(values.shape, values.dtype)], axis=1)


def sweep(blocks, make_scores, values, begin, finish, ahead=0):
    order = list(range(blocks))[::-1]
    current = [make_scores(order[0], span) for span in chunks(order[0] + 1)]
    early = [make_scores(b, span) for b in order[1 : 1 + ahead] for span in chunks(b + 1)]
    for i, b in enumerate(order):
        top = current[0].max(axis=1, keepdims=True)
        for s in current[1:]:
            top = jnp.maximum(top, s.max(axis=1, keepdims=True))
        top, total = begin(b, top)
        later = chunks(order[i + 1] + 1) if i + 1 < blocks else []
        following = early[: len(later)] if i < ahead else []
        early = early[len(later) :] if i < ahead else []
        later = [] if i < ahead else later
        for n, span in enumerate(chunks(b + 1)):
            if n < len(later):
                following.append(make_scores(order[i + 1], later[n]))
            s = current[n]
            wide = jnp.concatenate([top] * (s.shape[1] // top.shape[1]), axis=1)
            weights = jnp.exp2((s - wide) * TO_EXP2).astype(jnp.bfloat16)
            part = dot(weights, with_ones(rows_of(values, span)))
            total = part if total is None else total + part
        finish(b, top, total)
        current = following


def own_kernel(qk_own, *refs):
    v_any, refs = refs[:PARTS], refs[PARTS:]
    total_ref, top_ref, v_own, v_sem = refs
    blocks, _, rows, lanes = qk_own.shape
    each = blocks // PARTS
    loads = [
        pltpu.make_async_copy(part, v_own.at[pl.ds(i * each, each)], v_sem.at[i])
        for i, part in enumerate(v_any)
    ]
    for c in loads:
        c.start()
    row = lax.broadcasted_iota(jnp.int32, (rows, rows), 0)
    col = lax.broadcasted_iota(jnp.int32, (rows, rows), 1)
    on_diagonal = col <= row

    def make_scores(b, span):
        parts = []
        for j in range(*span):
            s = scores(qk_own[b, 0], qk_own[j, 1])
            parts.append(jnp.where(on_diagonal, s, MASKED) if j == b else s)
        return jnp.concatenate(parts, axis=1)

    def begin(b, top):
        if b == blocks - 1:
            for c in loads:
                c.wait()
        return jnp.broadcast_to(top, (rows, lanes)), None

    def finish(b, top, total):
        total_ref[b] = total
        top_ref[b] = top

    sweep(blocks, make_scores, [v_own.at[j] for j in range(blocks)], begin, finish, 1)


def attend_own(qk_own, v_own):
    blocks, _, rows, lanes = qk_own.shape
    return pl.pallas_call(
        own_kernel,
        in_specs=[VMEM] + [ANYWHERE] * PARTS,
        out_specs=[VMEM] * 2,
        out_shape=[
            jax.ShapeDtypeStruct((blocks, rows, 2 * lanes), jnp.float32),
            jax.ShapeDtypeStruct((blocks, rows, lanes), jnp.float32),
        ],
        scratch_shapes=[
            pltpu.VMEM((blocks, rows, lanes), jnp.bfloat16),
            pltpu.SemaphoreType.DMA((PARTS,)),
        ],
        **room(24, 10**9, MIB),
    )(qk_own, *[in_hbm(v) for v in v_own])


def other_kernel(core_ref, qk_own, k_other, total_ref, top_ref, *refs):
    v_any, v_other, refs = refs[:PARTS], refs[PARTS : 2 * PARTS], refs[2 * PARTS :]
    out, v_sem = refs
    blocks, _, rows, lanes = qk_own.shape
    each = blocks // PARTS
    stores = [
        pltpu.make_async_copy(part, out.at[pl.ds(i * each, each), 0], v_sem.at[i])
        for i, part in enumerate(v_any)
    ]
    for c in stores:
        c.start()
    beside = jnp.full((rows, rows), core_ref[0], jnp.int32) > 0

    def make_scores(b, span):
        parts = []
        for j in range(*span):
            s = scores(qk_own[b, 0], k_other[j])
            parts.append(jnp.where(beside, s, MASKED) if j == b else s)
        return jnp.concatenate(parts, axis=1)

    def begin(b, top):
        before = top_ref[b]
        top = jnp.maximum(before, top)
        shrink = jnp.exp2((before - top) * TO_EXP2)
        return top, total_ref[b] * jnp.concatenate([shrink, shrink], axis=1)

    def finish(b, top, total):
        out[b, 1] = (total[:, :lanes] / total[:, lanes:]).astype(jnp.bfloat16)

    values = [v_other[j // each].at[j % each] for j in range(blocks)]
    sweep(blocks, make_scores, values, begin, finish, 1)
    for c in stores:
        c.wait()


def attend_other(core, qk_own, k_other, total, top, v_own, v_other):
    blocks, _, rows, lanes = qk_own.shape
    return pl.pallas_call(
        other_kernel,
        in_specs=[SMEM] + [VMEM] * 4 + [ANYWHERE] * PARTS + [VMEM] * PARTS,
        out_specs=VMEM,
        out_shape=jax.ShapeDtypeStruct((blocks, 2, rows, lanes), jnp.bfloat16),
        scratch_shapes=[pltpu.SemaphoreType.DMA((PARTS,))],
        **room(24, 10**9, MIB),
    )(core, qk_own, k_other, total, top, *[in_hbm(v) for v in v_own], *v_other)


def to_chips(array):
    flat = array.reshape(array.shape[0], -1, array.shape[-1])
    moved = lax.all_to_all(flat, "chip", split_axis=0, concat_axis=0, tiled=True)
    return moved.reshape(array.shape)


def swap(array):
    return lax.ppermute(array, "core", [(0, 1), (1, 0)])


def per_device(gate_input, value_input, filter_taps, skip_gain, queries, keys):
    chip = lax.axis_index("chip")
    core = lax.axis_index("core").astype(jnp.int32).reshape(1)
    own = to_chips(pack(value_input, filter_taps, gate_input))
    forward, inverse = transform_tables(queries.shape[0])
    packed = pack_rest(queries, keys, forward)
    own, packed = lax.optimization_barrier((own, packed))
    qk_own = to_chips(packed[0])
    x_other, h_other = (swap(own[:, i]) for i in (0, 1))
    skip = lax.dynamic_slice(skip_gain, (chip * HEAD_DIM,), (HEAD_DIM,)).reshape(1, HEAD_DIM)
    v_own = convolve(core, own, x_other, h_other, skip, packed[1], inverse)
    qk_own, v_other = lax.optimization_barrier((qk_own, [swap(v) for v in v_own]))
    k_other = swap(qk_own[:, 1])
    total, top = attend_own(qk_own, v_own)
    back = to_chips(attend_other(core, qk_own, k_other, total, top, v_own, v_other))
    mixed, attended = unpack(back)
    return (mixed, attended)


def solution(mesh):
    ctx, tp = mesh.devices.shape
    fine = Mesh(mesh.devices.reshape(ctx // CORES, CORES, tp), ("chip", "core", "tp"))
    rows = P(("chip", "core"), "tp")
    return jax.shard_map(
        per_device,
        mesh=fine,
        in_specs=(rows, rows, rows, P("tp"), rows, rows),
        out_specs=(rows, rows),
        check_vma=False,
    )
```

```python
import functools
import math

import numpy as np

import jax
import jax.numpy as jnp
from jax import lax
from jax.experimental import pallas as pl
from jax.experimental.pallas import tpu as pltpu
from jax.sharding import Mesh, PartitionSpec as P

HEAD_DIM = 128
CORES = 2
SCALE = 1.0 / math.sqrt(HEAD_DIM)
MASKED = -1e30
PARTS = 1
TO_EXP2 = SCALE * math.log2(math.e)
MIB = 1024 * 1024


def transform_tables(rows):
    period = 2 * rows
    freq = np.arange(rows, dtype=np.float64)[:, None] + 0.5
    time = np.arange(period, dtype=np.float64)[None, :]
    angle = 2.0 * np.pi * freq * time / period
    first = angle[:, :rows]
    forward = np.concatenate([np.cos(first), -np.sin(first)], axis=0)
    later = angle[:, rows:].T
    inverse = np.concatenate([np.cos(later), -np.sin(later)], axis=1) / rows
    return jnp.asarray(forward, jnp.bfloat16), jnp.asarray(inverse, jnp.bfloat16)


def room(mib, flops=0, moved=0):
    return dict(
        compiler_params=pltpu.CompilerParams(vmem_limit_bytes=mib * MIB),
        cost_estimate=pl.CostEstimate(flops=flops, bytes_accessed=moved, transcendentals=0),
    )


VMEM = pl.BlockSpec(memory_space=pltpu.VMEM)
SMEM = pl.BlockSpec(memory_space=pltpu.SMEM)
ANYWHERE = pl.BlockSpec(memory_space=pl.ANY)


def pack_kernel(*refs, count, parts):
    inputs, out, held, made, sems, out_sem = (
        refs[:count],
        refs[count],
        refs[count + 1 : 2 * count + 1],
        refs[-3],
        refs[-2],
        refs[-1],
    )
    size = inputs[0].shape[0] // parts
    copies = [
        [
            pltpu.make_async_copy(
                ref.at[pl.ds(s * size, size)], buf.at[pl.ds(s * size, size)], sems.at[i, s]
            )
            for i, (ref, buf) in enumerate(zip(inputs, held))
        ]
        for s in range(parts)
    ]
    for part in copies:
        for c in part:
            c.start()
    stores = []
    for s, part in enumerate(copies):
        span = slice(s * size, (s + 1) * size)
        for i, c in enumerate(part):
            c.wait()
            for p in range(out.shape[0]):
                lanes = slice(p * HEAD_DIM, (p + 1) * HEAD_DIM)
                made[p, i, span] = held[i][span, lanes].astype(jnp.bfloat16)
            rows = pl.ds(s * size, size)
            stores.append(
                pltpu.make_async_copy(made.at[:, i, rows], out.at[:, i, rows], out_sem.at[i, s])
            )
            stores[-1].start()
    for c in stores:
        c.wait()


def pack(*arrays):
    rows, channels = arrays[0].shape
    chips = channels // HEAD_DIM
    count = len(arrays)
    parts = 2
    shape = (chips, count, rows, HEAD_DIM)
    return pl.pallas_call(
        functools.partial(pack_kernel, count=count, parts=parts),
        in_specs=[ANYWHERE] * count,
        out_specs=ANYWHERE,
        out_shape=jax.ShapeDtypeStruct(shape, jnp.bfloat16),
        scratch_shapes=[pltpu.VMEM(a.shape, a.dtype) for a in arrays]
        + [pltpu.VMEM(shape, jnp.bfloat16)]
        + [pltpu.SemaphoreType.DMA((count, parts))] * 2,
        **room(24, 0, 6 * MIB),
    )(*[in_hbm(a) for a in arrays])


def pack_rest_kernel(queries, keys, forward, out, forward_out):
    for p in range(out.shape[0]):
        lanes = slice(p * HEAD_DIM, (p + 1) * HEAD_DIM)
        out[p, 0] = queries[:, lanes]
        out[p, 1] = keys[:, lanes]
    forward_out[...] = forward[...]


def pack_rest(queries, keys, forward):
    rows, channels = queries.shape
    shape = (channels // HEAD_DIM, 2, rows, HEAD_DIM)
    return pl.pallas_call(
        pack_rest_kernel,
        in_specs=[VMEM] * 3,
        out_specs=[VMEM] * 2,
        out_shape=[
            jax.ShapeDtypeStruct(shape, jnp.bfloat16),
            jax.ShapeDtypeStruct(forward.shape, jnp.bfloat16),
        ],
        **room(16, 0, 2 * MIB),
    )(queries, keys, forward)


def unpack_kernel(back, mixed, attended, sems):
    copies = []
    for p in range(back.shape[0]):
        lanes = pl.ds(p * HEAD_DIM, HEAD_DIM)
        for i, out in enumerate((mixed, attended)):
            copies.append(pltpu.make_async_copy(back.at[p, i], out.at[:, lanes], sems.at[i, p]))
    for c in copies:
        c.start()
    for c in copies:
        c.wait()


def unpack(back):
    chips, count, rows, lanes = back.shape
    out = jax.ShapeDtypeStruct((rows, chips * lanes), jnp.bfloat16)
    return pl.pallas_call(
        unpack_kernel,
        in_specs=[VMEM],
        out_specs=[ANYWHERE] * count,
        out_shape=[out] * count,
        scratch_shapes=[pltpu.SemaphoreType.DMA((count, chips))],
        **room(8, 0, 2 * MIB),
    )(back)


def conv_kernel(core_ref, own, x_other, h_any, skip_ref, forward, inverse_any, *refs):
    outs, refs = refs[:PARTS], refs[PARTS:]
    x_spec, h_spec, y_spec, made, h_other, inverse, tap_sem, table_sem, out_sem = refs
    blocks, _, rows, lanes = own.shape
    core = core_ref[0]
    copy = pltpu.make_async_copy
    half = blocks // PARTS
    taps = [
        copy(h_any.at[pl.ds(s * half, half)], h_other.at[pl.ds(s * half, half)], tap_sem.at[s])
        for s in range(PARTS)
    ]
    table = copy(inverse_any, inverse, table_sem.at[0])
    for c in taps + [table]:
        c.start()

    def dot(a, b):
        return jnp.dot(a, b, preferred_element_type=jnp.float32)

    h_spec[0] = jnp.zeros((2 * rows, lanes), jnp.float32)
    h_spec[1] = jnp.zeros((2 * rows, lanes), jnp.float32)
    for side in range(2):
        for m in range(blocks):
            if side == 1 and m % half == 0:
                taps[m // half].wait()
            pair = (x_other[m], h_other[m]) if side else (own[m, 0], own[m, 1])
            both = jnp.concatenate(pair, axis=1)
            spectrum = dot(forward[...], both)
            x_spec[2 * m + side] = spectrum[:, :lanes]
            at = 2 * m + 2 + (core if side == 0 else 1 - core)
            h_spec[at] = spectrum[:, lanes:]

    step = 8
    row = lax.broadcasted_iota(jnp.int32, (step, lanes), 0)
    sign = 1.0 - 2.0 * (row % 2).astype(jnp.float32)

    @pl.loop(0, rows // step)
    def _(t):
        re = pl.ds(pl.multiple_of(t * step, step), step)
        im = pl.ds(pl.multiple_of(rows + t * step, step), step)
        xr = [x_spec[j, re] for j in range(2 * blocks)]
        xi = [x_spec[j, im] for j in range(2 * blocks)]
        yr = [None] * blocks
        yi = [None] * blocks
        for lag in range(blocks):
            for side in range(2):
                k = 2 * lag + 1 if side == 0 else 2 * lag + 2 * core
                hr = h_spec[k, re] + sign * h_spec[k + 1, im]
                hi = h_spec[k, im] - sign * h_spec[k + 1, re]
                for j in range(blocks - lag):
                    b = j + lag
                    ar, ai = xr[2 * j + side], xi[2 * j + side]
                    pr = ar * hr - ai * hi
                    pi = ar * hi + ai * hr
                    yr[b] = pr if yr[b] is None else yr[b] + pr
                    yi[b] = pi if yi[b] is None else yi[b] + pi
        for b in range(blocks):
            y_spec[re, b * lanes : (b + 1) * lanes] = yr[b]
            y_spec[im, b * lanes : (b + 1) * lanes] = yi[b]

    table.wait()
    skip = skip_ref[...]
    stores = []
    for m in range(blocks // 2):
        spectrum = y_spec[:, 2 * m * lanes : 2 * (m + 1) * lanes]
        convolved = dot(inverse[...], spectrum.astype(jnp.bfloat16))
        for s in range(2):
            b = 2 * m + s
            part = convolved[:, s * lanes : (s + 1) * lanes]
            direct = skip * own[b, 0].astype(jnp.float32)
            made[b] = (own[b, 2].astype(jnp.float32) * (part + direct)).astype(jnp.bfloat16)
            stores.append(copy(made.at[b], outs[b // half].at[b % half], out_sem.at[b]))
            stores[-1].start()
    for c in stores:
        c.wait()


def in_hbm(array):
    return pltpu.with_memory_space_constraint(array, pltpu.HBM)


def convolve(core, own, x_other, h_other, skip, forward, inverse):
    blocks, _, rows, lanes = own.shape
    return pl.pallas_call(
        conv_kernel,
        in_specs=[SMEM, VMEM, VMEM, ANYWHERE, VMEM, VMEM, ANYWHERE],
        out_specs=[pl.BlockSpec(memory_space=pltpu.HBM)] * PARTS,
        out_shape=[jax.ShapeDtypeStruct((blocks // PARTS, rows, lanes), jnp.bfloat16)] * PARTS,
        scratch_shapes=[
            pltpu.VMEM((2 * blocks, 2 * rows, lanes), jnp.float32),
            pltpu.VMEM((2 * blocks + 2, 2 * rows, lanes), jnp.float32),
            pltpu.VMEM((2 * rows, blocks * lanes), jnp.float32),
            pltpu.VMEM((blocks, rows, lanes), jnp.bfloat16),
            pltpu.VMEM((blocks, rows, lanes), jnp.bfloat16),
            pltpu.VMEM(inverse.shape, jnp.bfloat16),
            pltpu.SemaphoreType.DMA((PARTS,)),
            pltpu.SemaphoreType.DMA((1,)),
            pltpu.SemaphoreType.DMA((blocks,)),
        ],
        **room(24, 10**6, MIB),
    )(core, own, x_other, in_hbm(h_other), skip, forward, in_hbm(inverse))


def dot(a, b):
    return jnp.dot(a, b, preferred_element_type=jnp.float32)


def scores(q, k):
    return lax.dot_general(q, k, (((1,), (1,)), ((), ())), preferred_element_type=jnp.float32)


def chunks(count):
    return [(j, min(j + 2, count)) for j in range(0, count, 2)]


def rows_of(blocks, span):
    return jnp.concatenate([blocks[j][...] for j in range(*span)], axis=0)


def with_ones(values):
    return jnp.concatenate([values, jnp.ones(values.shape, values.dtype)], axis=1)


def sweep(blocks, make_scores, values, begin, finish, ahead=0):
    order = list(range(blocks))[::-1]
    current = [make_scores(order[0], span) for span in chunks(order[0] + 1)]
    early = [make_scores(b, span) for b in order[1 : 1 + ahead] for span in chunks(b + 1)]
    for i, b in enumerate(order):
        top = current[0].max(axis=1, keepdims=True)
        for s in current[1:]:
            top = jnp.maximum(top, s.max(axis=1, keepdims=True))
        top, total = begin(b, top)
        later = chunks(order[i + 1] + 1) if i + 1 < blocks else []
        following = early[: len(later)] if i < ahead else []
        early = early[len(later) :] if i < ahead else []
        later = [] if i < ahead else later
        for n, span in enumerate(chunks(b + 1)):
            if n < len(later):
                following.append(make_scores(order[i + 1], later[n]))
            s = current[n]
            wide = jnp.concatenate([top] * (s.shape[1] // top.shape[1]), axis=1)
            weights = jnp.exp2((s - wide) * TO_EXP2).astype(jnp.bfloat16)
            part = dot(weights, with_ones(rows_of(values, span)))
            total = part if total is None else total + part
        finish(b, top, total)
        current = following


def own_kernel(qk_own, *refs):
    v_any, refs = refs[:PARTS], refs[PARTS:]
    total_ref, top_ref, v_own, v_sem = refs
    blocks, _, rows, lanes = qk_own.shape
    each = blocks // PARTS
    loads = [
        pltpu.make_async_copy(part, v_own.at[pl.ds(i * each, each)], v_sem.at[i])
        for i, part in enumerate(v_any)
    ]
    for c in loads:
        c.start()
    row = lax.broadcasted_iota(jnp.int32, (rows, rows), 0)
    col = lax.broadcasted_iota(jnp.int32, (rows, rows), 1)
    on_diagonal = col <= row

    def make_scores(b, span):
        parts = []
        for j in range(*span):
            s = scores(qk_own[b, 0], qk_own[j, 1])
            parts.append(jnp.where(on_diagonal, s, MASKED) if j == b else s)
        return jnp.concatenate(parts, axis=1)

    def begin(b, top):
        if b == blocks - 1:
            for c in loads:
                c.wait()
        return jnp.broadcast_to(top, (rows, lanes)), None

    def finish(b, top, total):
        total_ref[b] = total
        top_ref[b] = top

    sweep(blocks, make_scores, [v_own.at[j] for j in range(blocks)], begin, finish, 1)


def attend_own(qk_own, v_own):
    blocks, _, rows, lanes = qk_own.shape
    return pl.pallas_call(
        own_kernel,
        in_specs=[VMEM] + [ANYWHERE] * PARTS,
        out_specs=[VMEM] * 2,
        out_shape=[
            jax.ShapeDtypeStruct((blocks, rows, 2 * lanes), jnp.float32),
            jax.ShapeDtypeStruct((blocks, rows, lanes), jnp.float32),
        ],
        scratch_shapes=[
            pltpu.VMEM((blocks, rows, lanes), jnp.bfloat16),
            pltpu.SemaphoreType.DMA((PARTS,)),
        ],
        **room(24, 10**9, MIB),
    )(qk_own, *[in_hbm(v) for v in v_own])


def other_kernel(core_ref, qk_own, k_other, total_ref, top_ref, *refs):
    v_any, v_other, refs = refs[:PARTS], refs[PARTS : 2 * PARTS], refs[2 * PARTS :]
    out, v_sem = refs
    blocks, _, rows, lanes = qk_own.shape
    each = blocks // PARTS
    stores = [
        pltpu.make_async_copy(part, out.at[pl.ds(i * each, each), 0], v_sem.at[i])
        for i, part in enumerate(v_any)
    ]
    for c in stores:
        c.start()
    beside = jnp.full((rows, rows), core_ref[0], jnp.int32) > 0

    def make_scores(b, span):
        parts = []
        for j in range(*span):
            s = scores(qk_own[b, 0], k_other[j])
            parts.append(jnp.where(beside, s, MASKED) if j == b else s)
        return jnp.concatenate(parts, axis=1)

    def begin(b, top):
        before = top_ref[b]
        top = jnp.maximum(before, top)
        shrink = jnp.exp2((before - top) * TO_EXP2)
        return top, total_ref[b] * jnp.concatenate([shrink, shrink], axis=1)

    def finish(b, top, total):
        out[b, 1] = (total[:, :lanes] / total[:, lanes:]).astype(jnp.bfloat16)

    values = [v_other[j // each].at[j % each] for j in range(blocks)]
    sweep(blocks, make_scores, values, begin, finish, 1)
    for c in stores:
        c.wait()


def attend_other(core, qk_own, k_other, total, top, v_own, v_other):
    blocks, _, rows, lanes = qk_own.shape
    return pl.pallas_call(
        other_kernel,
        in_specs=[SMEM] + [VMEM] * 4 + [ANYWHERE] * PARTS + [VMEM] * PARTS,
        out_specs=VMEM,
        out_shape=jax.ShapeDtypeStruct((blocks, 2, rows, lanes), jnp.bfloat16),
        scratch_shapes=[pltpu.SemaphoreType.DMA((PARTS,))],
        **room(24, 10**9, MIB),
    )(core, qk_own, k_other, total, top, *[in_hbm(v) for v in v_own], *v_other)


def to_chips(array):
    flat = array.reshape(array.shape[0], -1, array.shape[-1])
    moved = lax.all_to_all(flat, "chip", split_axis=0, concat_axis=0, tiled=True)
    return moved.reshape(array.shape)


def swap(array):
    return lax.ppermute(array, "core", [(0, 1), (1, 0)])


def per_device(gate_input, value_input, filter_taps, skip_gain, queries, keys):
    chip = lax.axis_index("chip")
    core = lax.axis_index("core").astype(jnp.int32).reshape(1)
    own = to_chips(pack(value_input, filter_taps, gate_input))
    forward, inverse = transform_tables(queries.shape[0])
    packed = pack_rest(queries, keys, forward)
    own, packed = lax.optimization_barrier((own, packed))
    qk_own = to_chips(packed[0])
    x_other, h_other = (swap(own[:, i]) for i in (0, 1))
    skip = lax.dynamic_slice(skip_gain, (chip * HEAD_DIM,), (HEAD_DIM,)).reshape(1, HEAD_DIM)
    v_own = convolve(core, own, x_other, h_other, skip, packed[1], inverse)
    qk_own, v_other = lax.optimization_barrier((qk_own, [swap(v) for v in v_own]))
    k_other = swap(qk_own[:, 1])
    total, top = attend_own(qk_own, v_own)
    back = to_chips(attend_other(core, qk_own, k_other, total, top, v_own, v_other))
    mixed, attended = unpack(back)
    return (mixed, attended)


def solution(mesh):
    ctx, tp = mesh.devices.shape
    fine = Mesh(mesh.devices.reshape(ctx // CORES, CORES, tp), ("chip", "core", "tp"))
    rows = P(("chip", "core"), "tp")
    return jax.shard_map(
        per_device,
        mesh=fine,
        in_specs=(rows, rows, rows, P("tp"), rows, rows),
        out_specs=(rows, rows),
        check_vma=False,
    )
```
